32 devices in a mesh: groups: 2 (over x), paths: 2 (over core), feats: 8 (over z, y).
Axes of the slice: x: 2, y: 2, z: 4, core: 2. Of those that a mesh axis runs over, the one named last changes fastest.
Arguments:
- factors: int32 [4096, 128], P(('groups', 'paths')), parts along dimension 0, may hold values from -8 to 8
- frequency: int32 [128, 65536], P(None, 'feats'), may hold values from -48 to 48
- phases: int32 [65536], P('feats'), may hold values from 0 to 1023
- amplitude: float32 [65536], P('feats'), as said below
- targets: float32 [32, 4096], P(None, ('groups', 'paths')), parts along dimension 1, may hold values from -6 to 6
- coeffs_init: float32 [32, 131072], P(None, ('groups', 'feats')), parts along dimension 1, may hold values from -6 to 6
Outputs:
- coeffs: float32 [32, 131072], P(None, ('groups', 'feats')), parts along dimension 1
- predicted: float32 [32, 4096], P(None, ('groups', 'paths')), parts along dimension 1
The draws below stay inside these ranges and needn't reach their ends.
There are 2 independent parts, one for each index of `groups`. The reference program is written for one: setup_inputs(seed, part) draws one part's arguments, and reference() takes and returns one part's arrays. A program takes and returns all parts, laid end to end along the dimension named above; an argument that names none is the same for every part. Nothing has to cross between parts.
Inputs may be any that keep to these rules, and one draw needn't show every extreme that they name: `amplitude`: positive feature weights.
All inputs are finite; a program needn't handle non-finite values.
Results may differ from the reference program's by a relative error of at most 0.00026.
Values sent between devices are 32-bit elements; how exact they have to be, the bound alone decides.
No kernel may reach another device: no remote copies, remote signals or barrier semaphores. Data moves between devices by JAX's collectives and lax.ppermute only.
A program may use at most 128 MiB of HBM per device.

```python
import math
import jax
import jax.numpy as jnp
from jax import lax

F = 65536
K = 128
V = 32
ITERS = 3
PATHS = 2048


def draw_amplitude(key, part):
    index = jnp.arange(F, dtype=jnp.float32)
    rising = jnp.exp(jnp.log(3.0) * index / F)
    spread = jnp.exp(jax.random.uniform(key, (F,), jnp.float32, minval=-1.2, maxval=1.2))
    return (spread * rising * jnp.sqrt(1.0 / F)).astype(jnp.float32)


def place_ends(array, key, smallest, top_value):
    longest = array.shape.index(max(array.shape))
    spots = []
    for shift in (0, 1):
        where = [jax.random.randint(jax.random.fold_in(key, axis), (), 0, length) for axis, length in enumerate(array.shape)]
        where[longest] = (where[longest] + shift) % array.shape[longest]
        spots.append(tuple(where))
    return array.at[spots[0]].set(smallest).at[spots[1]].set(top_value)


def block_scale(own_key, shape, cuts, low, high):
    loudness, own = 1.0, jax.random.fold_in(own_key, 6)
    for position, shards_of in cuts:
        steps = jnp.exp(jax.random.uniform(jax.random.fold_in(own, position), (shards_of,), jnp.float32, low / len(cuts), high / len(cuts)))
        loudness = loudness * jnp.repeat(steps, shape[position] // shards_of).reshape([-1 if axis == position else 1 for axis in range(len(shape))])
    return loudness


def bell_draw(own_key, dims, scale, bound, pieces=(), held_as=jnp.bfloat16):
    level = block_scale(own_key, dims, pieces, -0.22, 0.18) if pieces else 1.0
    values = jax.random.normal(own_key, dims, jnp.float32) * scale * level
    return jnp.minimum(jnp.maximum(values, -bound), bound).astype(held_as)


def setup_inputs(seed: int = 0, part: int = 0) -> dict:
    streams_of = jax.random.split(jax.random.key(seed), 7)
    part_keys = jax.random.split(jax.random.fold_in(streams_of[6], part), 7)
    factors = place_ends(jax.random.randint(part_keys[0], (PATHS, K), -8, 9), jax.random.fold_in(part_keys[0], 1), -8, 8).astype(jnp.int32)
    frequency = place_ends(jax.random.randint(streams_of[1], (K, F), 0 - 6144 // K, 6144 // K + 1), jax.random.fold_in(streams_of[1], 1), 0 - 6144 // K, (6144 // K + 1) - 1).astype(jnp.int32)
    phases = place_ends(jax.random.randint(streams_of[2], (F,), 0, 1024), jax.random.fold_in(streams_of[2], 1), 0, 1023).astype(jnp.int32)
    amplitude = draw_amplitude(jax.random.fold_in(streams_of[6], 71), part)
    targets = bell_draw(part_keys[4], (V, PATHS), 1.0, 6.0, ((1, 2),), jnp.float32)
    coeffs_init = bell_draw(part_keys[5], (V, F), 1.0, 6.0, ((1, 8),), jnp.float32)
    return {"factors": factors, "frequency": frequency, "phases": phases, "amplitude": amplitude, "targets": targets, "coeffs_init": coeffs_init}


huber_cap = 1.0
step_rate = 0.2
momentum = 0.9
epsilon = 1e-06

def build(factor_vals, freq_block, phase_block, amp_block):
    summed = jnp.dot(factor_vals, freq_block, precision=lax.Precision.HIGHEST, preferred_element_type=jnp.float32)
    return amp_block * jnp.cos(summed * 0.0025 + phase_block * (2.0 * math.pi / 1024.0))

def reference(factors, frequency, phases, amplitude, targets, coeffs_init):
    block_cols = min(F, 2048)
    nblocks = F // block_cols
    total_paths = targets.shape[1]
    factor_vals = factors.astype(jnp.float32)
    freq_blocks = jnp.transpose(frequency.astype(jnp.float32).reshape(K, nblocks, block_cols), (1, 0, 2))
    phase_blocks = phases.astype(jnp.float32).reshape(nblocks, block_cols)
    amp_blocks = amplitude.reshape(nblocks, block_cols)

    def feature_block(index):
        return build(factor_vals, freq_blocks[index], phase_blocks[index], amp_blocks[index])

    def predict(coeffs):
        coeff_blocks = jnp.transpose(coeffs.reshape(V, nblocks, block_cols), (1, 0, 2))

        def step(total, index):
            block = feature_block(index)
            part = lax.dot_general(coeff_blocks[index], block, (((1,), (1,)), ((), ())), precision=lax.Precision.HIGHEST, preferred_element_type=jnp.float32)
            return (total + part, None)
        total, _ = lax.scan(step, jnp.zeros((V, total_paths), jnp.float32), jnp.arange(nblocks, dtype=jnp.int32))
        return total
    coeffs = coeffs_init
    velocity = jnp.zeros_like(coeffs_init)
    predicted = predict(coeffs)
    for turn in range(ITERS):
        clipped = jnp.clip(predicted - targets, -huber_cap, huber_cap)

        def grad_step(carry, index):
            block = feature_block(index)
            return (carry, jnp.dot(clipped, block, precision=lax.Precision.HIGHEST, preferred_element_type=jnp.float32))
        _, grad_blocks = lax.scan(grad_step, jnp.float32(0.0), jnp.arange(nblocks, dtype=jnp.int32))
        gradient = jnp.transpose(grad_blocks, (1, 0, 2)).reshape(V, F)
        scale = jnp.sqrt(jnp.mean(gradient * gradient) + epsilon)
        velocity = momentum * velocity + gradient / scale
        coeffs = coeffs - step_rate * velocity
        predicted = predict(coeffs)
    return (coeffs, predicted)
```

```python
import functools
import math

import jax
import jax.numpy as jnp
from jax import lax
from jax.experimental import pallas as pl
from jax.experimental.pallas import tpu as pltpu
from jax.sharding import PartitionSpec as P

ITERS = 3

huber_cap = 1.0
step_rate = 0.2
momentum = 0.9
epsilon = 1e-06

f32 = jnp.float32
bf16 = jnp.bfloat16

SIN = None


def fit_sine(terms):
    import numpy as np

    nodes = np.cos(np.linspace(0, np.pi, 4000)) * 0.25
    square = nodes * nodes
    basis = np.stack([nodes * square**i for i in range(terms)], 1)
    found = np.linalg.lstsq(basis, np.sin(2 * np.pi * nodes), rcond=None)[0]
    return [float(np.float32(value)) for value in found]


SIN = fit_sine(4)
TURN = 0.0025 / (2.0 * math.pi)
NN = (((1,), (0,)), ((), ()))
NT = (((1,), (1,)), ((), ()))


def split(values):
    high = values.astype(bf16)
    return high, (values - high.astype(f32)).astype(bf16)


def cosine(turns):
    rest = turns - jnp.round(turns)
    place = 0.25 - jnp.abs(rest)
    square = place * place
    series = SIN[-1]
    for term in SIN[-2::-1]:
        series = series * square + term
    return series * place


def divisor(size, most):
    while size % most:
        most //= 2
    return most


def build_kernel(
    own_ref, other_ref, freq_ref, phase_ref, amp_ref, coeffs_ref, blank_high, blank_low, image_own, image_other, base_ref, high_ref, low_ref,
    freq_buf, freq_sem,
):
    paths, width = high_ref.shape
    half = paths // 2
    cols = freq_buf.shape[2]
    rows = divisor(half, 512)
    steps = width // cols
    count = coeffs_ref.shape[0]
    first = lax.axis_index("paths") * width
    image_own[...] = jnp.zeros_like(image_own)
    image_other[...] = jnp.zeros_like(image_other)

    def fetch(index, slot):
        source = pl.ds(pl.multiple_of(first + index * cols, cols), cols)
        return pltpu.make_async_copy(freq_ref.at[:, source], freq_buf.at[slot], freq_sem.at[slot])

    fetch(0, 0).start()

    def block(index, carry):
        slot = lax.rem(index, 2)

        @pl.when(index + 1 < steps)
        def _():
            fetch(index + 1, 1 - slot).start()

        fetch(index, slot).wait()
        span = pl.ds(pl.multiple_of(first + index * cols, cols), cols)
        target = pl.ds(pl.multiple_of(index * cols, cols), cols)
        freq = freq_buf[slot].astype(f32).astype(bf16)
        phase = phase_ref[:, span].astype(f32) * (1.0 / 1024.0)
        amp = amp_ref[:, span]
        base_ref[:, target] = coeffs_ref[:, span]
        start_high, start_low = split(coeffs_ref[:, span])
        start = jnp.concatenate([start_high, start_low], 0)
        for part in range(paths // rows):
            factor_ref, image_ref = (own_ref, image_own) if part * rows < half else (other_ref, image_other)
            place = pl.ds(part * rows % half, rows)
            factor = factor_ref[place, :].astype(f32).astype(bf16)
            summed = lax.dot_general(factor, freq, NN, preferred_element_type=f32)
            values = cosine(summed * TURN + phase) * amp
            high, low = split(values)
            high_ref[pl.ds(part * rows, rows), target] = high
            low_ref[pl.ds(part * rows, rows), target] = low
            main = lax.dot_general(start, high, NT, preferred_element_type=f32)
            rest = lax.dot_general(start_high, low, NT, preferred_element_type=f32)
            image_ref[:, place] += main[:count] + main[count:] + rest
        return carry

    lax.fori_loop(0, steps, block, 0)


def turn_kernel(weight, own_ref, other_ref, high_ref, low_ref, *refs):
    if weight is None:
        image_own, image_other, grad_ref, pair_ref = refs
    else:
        base_ref, before_ref, scale_ref, image_own, image_other, grad_ref, base_out, pair_ref = refs
    paths, width = high_ref.shape
    half = paths // 2
    count = own_ref.shape[0]
    cols = divisor(width, 1024)
    clip_high, clip_low = split(jnp.concatenate([own_ref[...], other_ref[...]], 1))
    clip_pair = jnp.concatenate([clip_high, clip_low], 0)
    squares = jnp.zeros((8, 128), f32)
    for index in range(width // cols):
        span = pl.ds(index * cols, cols)
        main = lax.dot_general(clip_pair, high_ref[:, span], NN, preferred_element_type=f32)
        rest = lax.dot_general(clip_high, low_ref[:, span], NN, preferred_element_type=f32)
        grad = main[:count] + main[count:] + rest
        grad_ref[:, span] = grad
        high, low = split(grad)
        pair_ref[:count, span] = high
        pair_ref[count:, span] = low
        for row in range(0, count, 8):
            for lane in range(0, cols, 128):
                tile = grad[row : row + 8, lane : lane + 128]
                squares = squares + tile * tile
        if weight is not None:
            base_out[:, span] = base_ref[:, span] - weight * (before_ref[:, span] / scale_ref[0:1, 0:1])
    for image_ref, start in ((image_own, 0), (image_other, half)):
        place = pl.ds(start, half)
        main = lax.dot_general(pair_ref[...], high_ref[place, :], NT, preferred_element_type=f32)
        rest = lax.dot_general(pair_ref[:count, :], low_ref[place, :], NT, preferred_element_type=f32)
        image = main[:count] + main[count:] + rest
        for lane in range(0, half, 128):
            image_ref[pl.ds(lane // 128 * count, count), :] = image[:, lane : lane + 128]
        image_ref[pl.ds(half // 128 * count, 8), :] = squares


def add_kernel(one_ref, other_ref, sum_ref):
    sum_ref[...] = one_ref[...] + other_ref[...]


def open_kernel(sum_ref, last_ref, targets_ref, clipped_out, predicted_out):
    predicted = sum_ref[...] + last_ref[...]
    predicted_out[...] = predicted
    clipped_out[...] = jnp.clip(predicted - targets_ref[...], -huber_cap, huber_cap)


def step_kernel(entries, sum_ref, last_ref, targets_ref, predicted_ref, *refs):
    if len(refs) == 5:
        tracked_ref = refs[0]
        refs = refs[1:]
    else:
        tracked_ref = None
    clipped_out, predicted_out, scale_out, tracked_out = refs
    count, half = targets_ref.shape
    tiles = half // 128
    end = pl.ds(tiles * count, 8)
    total = jnp.sum(sum_ref[end, :] + last_ref[end, :], axis=(0, 1), keepdims=True)
    scale = jnp.sqrt(total / entries + epsilon)
    scale_out[...] = jnp.broadcast_to(scale, (8, 128))
    for tile in range(tiles):
        place, span = pl.ds(tile * count, count), pl.ds(tile * 128, 128)
        tracked = (sum_ref[place, :] + last_ref[place, :]) / scale
        if tracked_ref is not None:
            tracked = momentum * tracked_ref[:, span] + tracked
        predicted = predicted_ref[:, span] - step_rate * tracked
        tracked_out[:, span] = tracked
        predicted_out[:, span] = predicted
        clipped_out[:, span] = jnp.clip(predicted - targets_ref[:, span], -huber_cap, huber_cap)


def close_kernel(weight, base_ref, other_base, grad_ref, other_grad, scale_ref, coeffs_out):
    width = base_ref.shape[1]
    core = lax.axis_index("paths")
    scale = scale_ref[0:1, 0:1]
    for start, base, grad in ((core, base_ref, grad_ref), (1 - core, other_base, other_grad)):
        span = pl.ds(pl.multiple_of(start * width, width), width)
        coeffs_out[:, span] = base[...] - weight * (grad[...] / scale)


def vmem(count):
    return [pl.BlockSpec(memory_space=pltpu.VMEM)] * count


def hbm(count):
    return [pl.BlockSpec(memory_space=pl.ANY)] * count


def held(array):
    return pltpu.with_memory_space_constraint(array, pltpu.VMEM)


def call(kernel, name, arguments, shapes, specs=None, scratch=(), megabytes=4, aliases={}):
    shapes = tuple(shape if not isinstance(shape, tuple) else jax.ShapeDtypeStruct(shape, f32) for shape in shapes)
    return pl.pallas_call(
        kernel,
        out_shape=shapes,
        in_specs=specs or vmem(len(arguments)),
        out_specs=tuple(vmem(len(shapes))),
        scratch_shapes=scratch,
        compiler_params=pltpu.CompilerParams(vmem_limit_bytes=megabytes * 2**20),
        input_output_aliases=aliases,
        name=name,
    )(*arguments)


def shards(sizes, factors, frequency, phases, amplitude, targets, coeffs_init):
    cores, chips = sizes["paths"], sizes["feats"]
    half = factors.shape[0]
    width = frequency.shape[1] // cores
    count = targets.shape[0]
    paths = half * cores
    entries = count * width * cores * chips
    hops = [1 << bit for bit in range(chips.bit_length() - 1)]

    def swap(array):
        return lax.ppermute(array, "paths", [(0, 1), (1, 0)])

    def add(one, other):
        return call(add_kernel, "add", (one, other), (one.shape,))[0]

    def all_chips(array):
        for step in range(len(hops)):
            pairs = [
                (way * chips + chip, way * chips + (chip ^ hops[(step + way) % len(hops)]))
                for way in range(cores)
                for chip in range(chips)
            ]
            last = lax.ppermute(array, ("paths", "feats"), pairs)
            if step < len(hops) - 1:
                array = add(array, last)
        return array, last

    cols = divisor(width, 512)
    small, wide = (count, half), (count, width)
    blanks = [
        pl.pallas_call(
            lambda out: None,
            out_shape=pltpu.VMEM((paths, width), bf16),
            out_specs=vmem(1)[0],
            compiler_params=pltpu.CompilerParams(vmem_limit_bytes=2**20),
            name=name,
        )()
        for name in ("blank_high", "blank_low")
    ]
    blank_high, blank_low = blanks
    image_own, image_other, base, high, low = call(
        build_kernel,
        "build",
        (factors, swap(factors), frequency, phases[None], amplitude[None], coeffs_init, held(blank_high), held(blank_low)),
        (small, small, wide, pltpu.VMEM((paths, width), bf16), pltpu.VMEM((paths, width), bf16)),
        vmem(2) + hbm(1) + vmem(5),
        [pltpu.VMEM((2,) + (frequency.shape[0], cols), frequency.dtype), pltpu.SemaphoreType.DMA((2,))],
        20,
        {6: 3, 7: 4},
    )
    array, last = all_chips(add(image_own, swap(image_other)))
    clipped, predicted = call(open_kernel, "open", (array, last, targets), (small, small))
    extent = (count * half // 128 + 8, 128)
    weights = [step_rate * sum(momentum**later for later in range(ITERS - turn)) for turn in range(ITERS)]
    tracked = ()
    for turn in range(ITERS):
        arguments = (clipped, swap(clipped), held(high), held(low))
        shapes = (extent, extent, wide)
        if turn:
            arguments += (base, grad, scale)
            shapes += (wide,)
        image_own, image_other, grad, *rest = call(
            functools.partial(turn_kernel, weights[turn - 1] if turn else None),
            "turn",
            arguments,
            shapes,
            None,
            [pltpu.VMEM((2 * count, width), bf16)],
            20,
        )
        if turn:
            base = rest[0]
        array, last = all_chips(add(image_own, swap(image_other)))
        clipped, predicted, scale, *tracked = call(
            functools.partial(step_kernel, entries),
            "step",
            (array, last, targets, predicted, *tracked),
            (small, small, (8, 128), small),
        )
    coeffs = call(
        functools.partial(close_kernel, weights[-1]),
        "close",
        (base, swap(base), grad, swap(grad), scale),
        ((count, width * cores),),
        None,
        (),
        8,
    )[0]
    return (coeffs, predicted)


def solution(mesh):
    return jax.shard_map(
        functools.partial(shards, dict(mesh.shape)),
        mesh=mesh,
        in_specs=(
            P(("groups", "paths"), None),
            P(None, "feats"),
            P("feats"),
            P("feats"),
            P(None, ("groups", "paths")),
            P(None, ("groups", "feats")),
        ),
        out_specs=(P(None, ("groups", "feats")), P(None, ("groups", "paths"))),
        check_vma=False,
    )
```

```python
import functools
import math

import jax
import jax.numpy as jnp
import numpy as np
from jax import lax
from jax.experimental import pallas as pl
from jax.experimental.pallas import tpu as pltpu
from jax.sharding import PartitionSpec as P

ITERS = 3

huber_cap = 1.0
step_rate = 0.2
momentum = 0.9
epsilon = 1e-06

f32 = jnp.float32
bf16 = jnp.bfloat16
f8 = jnp.float8_e4m3fn
NN = (((1,), (0,)), ((), ()))
NT = (((1,), (1,)), ((), ()))
TURN = 0.0025 / (2.0 * math.pi)


def fit_sine(terms):
    nodes = np.cos(np.linspace(0, np.pi, 4000)) * 0.25
    square = nodes * nodes
    basis = np.stack([nodes * square**i for i in range(terms)], 1)
    return np.linalg.lstsq(basis, np.sin(2 * np.pi * nodes), rcond=None)[0]


SINE = fit_sine(4)
TOP = float(SINE[-1])
SERIES = [float(term / SINE[-1]) for term in SINE]
LOW = 2.0**22
CLIP = 256.0


def split(values):
    high = values.astype(bf16)
    return high, (values - high.astype(f32)).astype(bf16)


def cosine(turns):
    place = 0.25 - jnp.abs(turns - jnp.round(turns))
    square = place * place
    series = square + SERIES[-2]
    for term in SERIES[-3::-1]:
        series = series * square + term
    return series * place


def divisor(size, most):
    while size % most:
        most //= 2
    return most


def build_kernel(
    own_ref, other_ref, freq_ref, phase_ref, amp_ref, coeffs_ref, blank_high, blank_low,
    image_own, image_other, amp_out, high_ref, low_ref,
    factor_buf, freq_buf, freq_sem,
):
    paths, width = high_ref.shape
    half = paths // 2
    risks = freq_buf.shape[1]
    cols = freq_buf.shape[2]
    rows = divisor(half, 512)
    steps = width // cols
    count = coeffs_ref.shape[0]
    first = lax.axis_index("paths") * width

    def fetch(index, slot):
        source = pl.ds(pl.multiple_of(first + index * cols, cols), cols)
        return pltpu.make_async_copy(freq_ref.at[:, source], freq_buf.at[slot], freq_sem.at[slot])

    fetch(0, 0).start()
    image_own[...] = jnp.zeros_like(image_own)
    image_other[...] = jnp.zeros_like(image_other)
    extra = factor_buf.shape[1] - risks
    ones = (lax.broadcasted_iota(jnp.int32, (half, extra), 1) < 3).astype(f32).astype(bf16)
    for start, ref in ((0, own_ref), (half, other_ref)):
        factor_buf[pl.ds(start, half), :risks] = ref[...].astype(f32).astype(bf16)
        factor_buf[pl.ds(start, half), risks:] = ones

    def block(index, carry):
        slot = lax.rem(index, 2)

        @pl.when(index + 1 < steps)
        def _():
            fetch(index + 1, 1 - slot).start()

        fetch(index, slot).wait()
        span = pl.ds(pl.multiple_of(first + index * cols, cols), cols)
        target = pl.ds(pl.multiple_of(index * cols, cols), cols)
        freq = freq_buf[slot].astype(f32).astype(bf16)
        phase = phase_ref[:, span].astype(f32) * (1.0 / (1024.0 * TURN))
        piece_high, rest = split(phase)
        rest = phase - piece_high.astype(f32)
        piece_middle, piece_low = split(rest)
        row = lax.broadcasted_iota(jnp.int32, (extra, cols), 0)
        pieces = jnp.where(
            row == 0,
            piece_high.astype(f32),
            jnp.where(row == 1, piece_middle.astype(f32), jnp.where(row == 2, piece_low.astype(f32), 0.0)),
        ).astype(bf16)
        freq = jnp.concatenate([freq, pieces], 0)
        amp = amp_ref[:, span] * TOP
        amp_out[:, target] = amp
        coeffs = coeffs_ref[:, span]
        start_high, start_low = split(coeffs * amp)
        start = jnp.concatenate([start_high, start_low], 0)
        for part in range(paths // rows):
            place = pl.ds(part * rows, rows)
            image_ref = image_own if part * rows < half else image_other
            summed = lax.dot_general(factor_buf[place, :], freq, NN, preferred_element_type=f32)
            values = cosine(summed * TURN)
            high = values.astype(bf16)
            rest = values - high.astype(f32)
            low = rest.astype(bf16)
            high_ref[place, target] = high
            low_ref[place, target] = (rest * LOW).astype(f8)
            main = lax.dot_general(start, high, NT, preferred_element_type=f32)
            rest = lax.dot_general(start_high, low, NT, preferred_element_type=f32)
            image_ref[:, pl.ds(part * rows % half, rows)] += main[:count] + main[count:] + rest
        return carry

    lax.fori_loop(0, steps, block, 0)


def gradient_of(clipped, high_ref, low_ref, place, span):
    count = clipped.shape[0]
    pair = jnp.concatenate(split(clipped), 0)
    main = lax.dot_general(pair, high_ref[place, span], NN, preferred_element_type=f32)
    coarse = (clipped * CLIP).astype(f8)
    rest = lax.dot_general(coarse, low_ref[place, span], NN, preferred_element_type=f32)
    return main[:count] + main[count:] + rest * (1.0 / (CLIP * LOW))


def image_of(pair_ref, coarse_ref, level, high_ref, low_ref, place, image_ref):
    count = pair_ref.shape[0] // 2
    main = lax.dot_general(pair_ref[...], high_ref[place, :], NT, preferred_element_type=f32)
    rest = lax.dot_general(coarse_ref[...], low_ref[place, :], NT, preferred_element_type=f32)
    image = main[:count] + main[count:] + rest * (level * (1.0 / LOW))
    for tile in range(image.shape[1] // 128):
        image_ref[pl.ds(tile * count, count), :] = image[:, tile * 128 : tile * 128 + 128]


def own_kernel(clipped_ref, high_ref, low_ref, partial_out):
    paths, width = high_ref.shape
    cols = divisor(width, 1024)
    for index in range(width // cols):
        span = pl.ds(index * cols, cols)
        partial_out[:, span] = gradient_of(clipped_ref[...], high_ref, low_ref, pl.ds(0, paths // 2), span)


def rest_kernel(
    clipped_ref, high_ref, low_ref, partial_ref, amp_ref, grad_out, pair_out, coarse_out, image_out, notes_out
):
    paths, width = high_ref.shape
    half = paths // 2
    count = clipped_ref.shape[0]
    cols = divisor(width, 1024)
    squares = jnp.zeros((8, 128), f32)
    largest = jnp.zeros((count, 128), f32)
    for index in range(width // cols):
        span = pl.ds(index * cols, cols)
        share = gradient_of(clipped_ref[...], high_ref, low_ref, pl.ds(half, half), span)
        amp = amp_ref[:, span]
        grad = (partial_ref[:, span] + share) * amp
        grad_out[:, span] = grad
        pushed = grad * amp
        high, low = split(pushed)
        pair_out[:count, span] = high
        pair_out[count:, span] = low
        for lane in range(0, cols, 128):
            largest = jnp.maximum(largest, jnp.abs(pushed[:, lane : lane + 128]))
            for row in range(0, count, 8):
                tile = grad[row : row + 8, lane : lane + 128]
                squares = squares + tile * tile
    level = jnp.maximum(jnp.max(largest, axis=1, keepdims=True), 1e-30) * (1.0 / 240.0)
    for index in range(width // cols):
        span = pl.ds(index * cols, cols)
        coarse_out[:, span] = (pair_out[:count, span].astype(f32) * (1.0 / level)).astype(f8)
    image_of(pair_out, coarse_out, level, high_ref, low_ref, pl.ds(half, half), image_out)
    image_out[pl.ds(count * half // 128, 8), :] = squares
    notes_out[:8, :] = squares
    notes_out[8:, :] = jnp.broadcast_to(level, (count, 128))


def image_kernel(pair_ref, coarse_ref, notes_ref, high_ref, low_ref, image_out):
    half = high_ref.shape[0] // 2
    image_of(pair_ref, coarse_ref, notes_ref[8:, :1], high_ref, low_ref, pl.ds(0, half), image_out)
    image_out[pl.ds(pair_ref.shape[0] // 2 * half // 128, 8), :] = notes_ref[:8, :]


def start_kernel(own_ref, other_ref, front_out, back_out):
    count, half = own_ref.shape
    tiles = half // 128
    for tile in range(tiles):
        out = front_out if tile < tiles // 2 else back_out
        span = pl.ds(tile * 128, 128)
        out[pl.ds(tile % (tiles // 2) * count, count), :] = own_ref[:, span] + other_ref[:, span]


def join_kernel(own_ref, other_ref, front_out, back_out):
    middle, end = back_out.shape[0], 2 * back_out.shape[0]
    front_out[:middle, :] = own_ref[:middle, :] + other_ref[:middle, :]
    front_out[middle:, :] = own_ref[end:, :] + other_ref[end:, :]
    back_out[...] = own_ref[middle:end, :] + other_ref[middle:end, :]


def add_kernel(one_ref, other_ref, sum_ref):
    sum_ref[...] = one_ref[...] + other_ref[...]


def places(targets_ref, front, back):
    count, half = targets_ref.shape
    tiles = half // 128
    for tile in range(tiles):
        refs = front if tile < tiles // 2 else back
        yield pl.ds(tile * 128, 128), refs, pl.ds(tile % (tiles // 2) * count, count)


def open_kernel(front, front_last, back, back_last, targets_ref, clipped_out, predicted_out):
    for span, (one, other), rows in places(targets_ref, (front, front_last), (back, back_last)):
        predicted = one[rows, :] + other[rows, :]
        predicted_out[:, span] = predicted
        clipped_out[:, span] = jnp.clip(predicted - targets_ref[:, span], -huber_cap, huber_cap)


def step_kernel(entries, front, front_last, back, back_last, targets_ref, predicted_ref, *refs):
    tracked_ref = refs[0] if len(refs) == 5 else None
    clipped_out, predicted_out, inverse_out, tracked_out = refs[-4:]
    end = pl.ds(back.shape[0], 8)
    total = jnp.sum(front[end, :] + front_last[end, :], axis=(0, 1), keepdims=True)
    inverse = 1.0 / jnp.sqrt(total / entries + epsilon)
    inverse_out[...] = jnp.broadcast_to(inverse, (8, 128))
    for span, (one, other), rows in places(targets_ref, (front, front_last), (back, back_last)):
        tracked = (one[rows, :] + other[rows, :]) * inverse
        if tracked_ref is not None:
            tracked = momentum * tracked_ref[:, span] + tracked
        predicted = predicted_ref[:, span] - step_rate * tracked
        tracked_out[:, span] = tracked
        predicted_out[:, span] = predicted
        clipped_out[:, span] = jnp.clip(predicted - targets_ref[:, span], -huber_cap, huber_cap)


def sum_kernel(weights, *refs):
    total = jnp.zeros_like(refs[-1])
    for weight, grad_ref, inverse_ref in zip(weights, refs[:-1:2], refs[1:-1:2]):
        total = total + (weight * inverse_ref[0:1, 0:1]) * grad_ref[...]
    refs[-1][...] = total


def close_kernel(weight, coeffs_ref, taken_ref, other_taken, grad_ref, other_grad, inverse_ref, coeffs_out):
    width = taken_ref.shape[1]
    core = lax.axis_index("paths")
    factor = weight * inverse_ref[0:1, 0:1]
    for start, taken, grad in ((core, taken_ref, grad_ref), (1 - core, other_taken, other_grad)):
        span = pl.ds(pl.multiple_of(start * width, width), width)
        coeffs_out[:, span] = coeffs_ref[:, span] - (taken[...] + factor * grad[...])


def vmem(count):
    return [pl.BlockSpec(memory_space=pltpu.VMEM)] * count


def held(array):
    return pltpu.with_memory_space_constraint(array, pltpu.VMEM)


def call(kernel, name, arguments, shapes, specs=None, scratch=(), megabytes=4, aliases={}):
    shapes = tuple(shape if not isinstance(shape, tuple) else jax.ShapeDtypeStruct(shape, f32) for shape in shapes)
    return pl.pallas_call(
        kernel,
        out_shape=shapes,
        in_specs=specs or vmem(len(arguments)),
        out_specs=tuple(vmem(len(shapes))),
        scratch_shapes=scratch,
        compiler_params=pltpu.CompilerParams(vmem_limit_bytes=megabytes * 2**20),
        input_output_aliases=aliases,
        name=name,
    )(*arguments)


def shards(sizes, factors, frequency, phases, amplitude, targets, coeffs_init):
    cores, chips = sizes["paths"], sizes["feats"]
    half, risks = factors.shape
    width = frequency.shape[1] // cores
    count = targets.shape[0]
    paths = half * cores
    entries = count * width * cores * chips
    hops = [1 << bit for bit in range(chips.bit_length() - 1)]

    def swap(array):
        return lax.ppermute(array, "paths", [(0, 1), (1, 0)])

    def add(one, other):
        return call(add_kernel, "add", (one, other), (one.shape,))[0]

    def all_chips(front, back):
        orders = hops, hops[1::-1] + hops[2:]
        sums = [front, back]
        for step in range(len(hops)):
            lasts = [
                lax.ppermute(array, "feats", [(chip, chip ^ order[step]) for chip in range(chips)])
                for array, order in zip(sums, orders)
            ]
            if step < len(hops) - 1:
                sums = [add(array, last) for array, last in zip(sums, lasts)]
        return sums[0], lasts[0], sums[1], lasts[1]

    cols = divisor(width, 512)
    small, wide, row = (count, half), (count, width), (1, width)
    extent = count * half // 128
    middle = extent // 2
    features = pltpu.VMEM((paths, width), bf16), pltpu.VMEM((paths, width), f8)
    blanks = [
        pl.pallas_call(
            lambda out: None,
            out_shape=feature,
            out_specs=vmem(1)[0],
            compiler_params=pltpu.CompilerParams(vmem_limit_bytes=2**20),
            name=name,
        )()
        for name, feature in zip(("blank_high", "blank_low"), features)
    ]
    image_own, image_other, amp, high, low = call(
        build_kernel,
        "build",
        (factors, swap(factors), frequency, phases[None], amplitude[None], coeffs_init, held(blanks[0]), held(blanks[1])),
        (small, small, row, *features),
        vmem(2) + [pl.BlockSpec(memory_space=pl.ANY)] + vmem(5),
        [
            pltpu.VMEM((paths, 2 * risks), bf16),
            pltpu.VMEM((2, risks, cols), frequency.dtype),
            pltpu.SemaphoreType.DMA((2,)),
        ],
        20,
        {6: 3, 7: 4},
    )
    sums = all_chips(*call(start_kernel, "start", (image_own, swap(image_other)), ((middle, 128), (middle, 128))))
    clipped, predicted = call(open_kernel, "open", (*sums, targets), (small, small))
    weights = [step_rate * sum(momentum**later for later in range(ITERS - turn)) for turn in range(ITERS)]
    tracked = ()
    grads, inverses = [], []
    for turn in range(ITERS):
        partial = call(own_kernel, "own", (clipped, held(high), held(low)), (wide,), None, (), 20)[0]
        pieces = jax.ShapeDtypeStruct((2 * count, width), bf16), jax.ShapeDtypeStruct(wide, f8)
        grad, pair, coarse, image_other, notes = call(
            rest_kernel,
            "rest",
            (swap(clipped), held(high), held(low), partial, amp),
            (wide, *pieces, (extent + 8, 128), (count + 8, 128)),
            None,
            (),
            20,
        )
        image_own = call(
            image_kernel, "image", (pair, coarse, notes, held(high), held(low)), ((extent + 8, 128),), None, (), 20
        )[0]
        halves = call(join_kernel, "join", (image_own, swap(image_other)), ((middle + 8, 128), (middle, 128)))
        clipped, predicted, inverse, *tracked = call(
            functools.partial(step_kernel, entries),
            "step",
            (*all_chips(*halves), targets, predicted, *tracked),
            (small, small, (8, 128), small),
        )
        grads.append(grad)
        inverses.append(inverse)
    before = [array for pair in zip(grads[:-1], inverses[:-1]) for array in pair]
    taken = call(functools.partial(sum_kernel, weights[:-1]), "sum", before, (wide,))[0]
    coeffs = call(
        functools.partial(close_kernel, weights[-1]),
        "close",
        (coeffs_init, taken, swap(taken), grads[-1], swap(grads[-1]), inverses[-1]),
        ((count, width * cores),),
        None,
        (),
        8,
    )[0]
    return (coeffs, predicted)


def solution(mesh):
    return jax.shard_map(
        functools.partial(shards, dict(mesh.shape)),
        mesh=mesh,
        in_specs=(
            P(("groups", "paths"), None),
            P(None, "feats"),
            P("feats"),
            P("feats"),
            P(None, ("groups", "paths")),
            P(None, ("groups", "feats")),
        ),
        out_specs=(P(None, ("groups", "feats")), P(None, ("groups", "paths"))),
        check_vma=False,
    )
```

```python
import functools
import math

import jax
import jax.numpy as jnp
import numpy as np
from jax import lax
from jax.experimental import pallas as pl
from jax.experimental.pallas import tpu as pltpu
from jax.sharding import PartitionSpec as P

ITERS = 3

huber_cap = 1.0
step_rate = 0.2
momentum = 0.9
epsilon = 1e-06

f32 = jnp.float32
bf16 = jnp.bfloat16
f8 = jnp.float8_e4m3fn
NN = (((1,), (0,)), ((), ()))
NT = (((1,), (1,)), ((), ()))
TURN = 0.0025 / (2.0 * math.pi)


def fit_half_angle():
    rest = np.cos(np.linspace(0, np.pi, 4001)) * 0.5
    target = np.cos(np.pi * rest)
    basis = np.stack([rest ** (2 * i) for i in range(4)], 1)
    weight = np.abs(target) + 1e-3
    return np.linalg.lstsq(basis * weight[:, None], target * weight, rcond=None)[0]


HALF = fit_half_angle()
TOP = float(2.0 * HALF[-1] ** 2)
SERIES = [float(term / HALF[-1]) for term in HALF]
LOW = 2.0**15
CLIP = 256.0
GRANT = 20


def split(values):
    high = values.astype(bf16)
    return high, (values - high.astype(f32)).astype(bf16)


def cosine(turns):
    rest = turns - jnp.round(turns)
    square = rest * rest
    series = square + SERIES[2]
    series = series * square + SERIES[1]
    series = series * square + SERIES[0]
    return series * series - 1.0 / TOP


def divisor(size, most):
    while size % most:
        most //= 2
    return most


def padded(factors, width):
    rows, risks = factors.shape
    ones = (lax.broadcasted_iota(jnp.int32, (rows, width - risks), 1) < 3).astype(f32)
    return jnp.concatenate([factors.astype(f32).astype(bf16), ones.astype(bf16)], 1)


def prepare_kernel(
    own_ref, freq_ref, phase_ref, amp_ref, coeffs_ref, factor_out, freq_out, start_out, amp_out,
    own_buf, freq_buf, phase_buf, amp_buf, coeffs_buf, whole_sem, freq_sem,
):
    risks = own_ref.shape[1]
    count = coeffs_ref.shape[0]
    steps, _, cols = freq_buf.shape
    extra = freq_out.shape[0] - risks
    first = lax.axis_index("paths") * cols * steps

    def fetch(index):
        source = pl.ds(pl.multiple_of(first + index * cols, cols), cols)
        return pltpu.make_async_copy(freq_ref.at[:, source], freq_buf.at[index], freq_sem.at[index])

    mine = pl.ds(pl.multiple_of(first, cols), cols * steps)
    wholes = [
        pltpu.make_async_copy(source, target, whole_sem.at[number])
        for number, (source, target) in enumerate(
            (
                (phase_ref.at[:, mine], phase_buf),
                (amp_ref.at[:, mine], amp_buf),
                (coeffs_ref.at[:, mine], coeffs_buf),
                (own_ref, own_buf),
            )
        )
    ]
    for copy in wholes:
        copy.start()
    for index in range(steps):
        fetch(index).start()
    for copy in wholes:
        copy.wait()
    factor_out[...] = padded(own_buf[...], factor_out.shape[1])
    row = lax.broadcasted_iota(jnp.int32, (extra, cols), 0)
    for index in range(steps):
        span = pl.ds(index * cols, cols)
        phase = phase_buf[:, span].astype(f32) * (1.0 / (1024.0 * TURN))
        piece_high = phase.astype(bf16).astype(f32)
        piece_middle = (phase - piece_high).astype(bf16).astype(f32)
        piece_low = phase - piece_high - piece_middle
        pieces = jnp.where(row == 0, piece_high, jnp.where(row == 1, piece_middle, jnp.where(row == 2, piece_low, 0.0)))
        freq_out[risks:, span] = pieces.astype(bf16)
        amp = amp_buf[:, span] * TOP
        amp_out[:, span] = amp
        start_high, start_low = split(coeffs_buf[:, span] * amp)
        start_out[:count, span] = start_high
        start_out[count:, span] = start_low
    for index in range(steps):
        fetch(index).wait()
        freq_out[:risks, pl.ds(index * cols, cols)] = freq_buf[index].astype(f32).astype(bf16)


def build_kernel(
    own_ref, other_ref, freq_ref, start_ref, blank_high, blank_low, image_own, image_other, high_ref, low_ref, other_buf
):
    paths, width = high_ref.shape
    half = paths // 2
    cols = divisor(width, 2048)
    rows = divisor(half, 512)
    count = start_ref.shape[0] // 2
    other_buf[...] = padded(other_ref[...], other_buf.shape[1])

    def add_image(part, index, high, low):
        start = start_ref[:, pl.ds(index * cols, cols)]
        main = lax.dot_general(start, high, NT, preferred_element_type=f32)
        rest = lax.dot_general(low, start[:count], NT, preferred_element_type=f32)
        image = main[:count] + main[count:] + rest.T
        image_ref = image_own if part * rows < half else image_other
        place = pl.ds(part * rows % half, rows)
        if index:
            image = image + image_ref[:, place]
        image_ref[:, place] = image

    def sums_of(stage):
        index, part = stage
        factor_ref = own_ref if part * rows < half else other_buf
        factors = factor_ref[pl.ds(part * rows % half, rows), :]
        return lax.dot_general(factors, freq_ref[:, pl.ds(index * cols, cols)], NN, preferred_element_type=f32)

    stages = [(index, part) for index in range(width // cols) for part in range(paths // rows)]
    summed = sums_of(stages[0])
    before = None
    for number, (index, part) in enumerate(stages):
        if number + 1 < len(stages):
            summed_after = sums_of(stages[number + 1])
        place, span = pl.ds(part * rows, rows), pl.ds(index * cols, cols)
        values = cosine(summed * TURN)
        high = values.astype(bf16)
        rest = values - high.astype(f32)
        high_ref[place, span] = high
        low_ref[place, span] = (rest * LOW).astype(f8)
        if before is not None:
            add_image(*before)
        before = part, index, high, rest.astype(bf16)
        summed = summed_after
    add_image(*before)


def gradient_of(clipped, high_ref, low_ref, place, span):
    count = clipped.shape[0]
    pair = jnp.concatenate(split(clipped), 0)
    main = lax.dot_general(pair, high_ref[place, span], NN, preferred_element_type=f32)
    coarse = (clipped * CLIP).astype(f8)
    rest = lax.dot_general(coarse, low_ref[place, span], NN, preferred_element_type=f32)
    return main[:count] + main[count:] + rest * (1.0 / (CLIP * LOW))


def image_of(pair_ref, coarse_ref, level, high_ref, low_ref, place, image_ref):
    count = pair_ref.shape[0] // 2
    main = lax.dot_general(pair_ref[...], high_ref[place, :], NT, preferred_element_type=f32)
    rest = lax.dot_general(coarse_ref[...], low_ref[place, :], NT, preferred_element_type=f32)
    image = main[:count] + main[count:] + rest * (level * (1.0 / LOW))
    for tile in range(image.shape[1] // 128):
        image_ref[pl.ds(tile * count, count), :] = image[:, tile * 128 : tile * 128 + 128]


def own_kernel(clipped_ref, high_ref, low_ref, partial_out):
    paths, width = high_ref.shape
    cols = divisor(width, 1024)
    for index in range(width // cols):
        span = pl.ds(index * cols, cols)
        partial_out[:, span] = gradient_of(clipped_ref[...], high_ref, low_ref, pl.ds(0, paths // 2), span)


def rest_kernel(
    clipped_ref, high_ref, low_ref, partial_ref, amp_ref, grad_out, pair_out, coarse_out, image_out, notes_out
):
    paths, width = high_ref.shape
    half = paths // 2
    count = clipped_ref.shape[0]
    cols = divisor(width, 1024)
    squares = jnp.zeros((8, 128), f32)
    largest = jnp.zeros((count, 128), f32)
    for index in range(width // cols):
        span = pl.ds(index * cols, cols)
        share = gradient_of(clipped_ref[...], high_ref, low_ref, pl.ds(half, half), span)
        amp = amp_ref[:, span]
        grad = (partial_ref[:, span] + share) * amp
        grad_out[:, span] = grad
        pushed = grad * amp
        high, low = split(pushed)
        pair_out[:count, span] = high
        pair_out[count:, span] = low
        for lane in range(0, cols, 128):
            largest = jnp.maximum(largest, jnp.abs(pushed[:, lane : lane + 128]))
            for row in range(0, count, 8):
                tile = grad[row : row + 8, lane : lane + 128]
                squares = squares + tile * tile
    level = jnp.maximum(jnp.max(largest, axis=1, keepdims=True), 1e-30) * (1.0 / 240.0)
    for index in range(width // cols):
        span = pl.ds(index * cols, cols)
        coarse_out[:, span] = (pair_out[:count, span].astype(f32) * (1.0 / level)).astype(f8)
    image_of(pair_out, coarse_out, level, high_ref, low_ref, pl.ds(half, half), image_out)
    image_out[pl.ds(count * half // 128, 8), :] = squares
    notes_out[:8, :] = squares
    notes_out[8:, :] = jnp.broadcast_to(level, (count, 128))


def image_kernel(pair_ref, coarse_ref, notes_ref, high_ref, low_ref, image_out):
    half = high_ref.shape[0] // 2
    image_of(pair_ref, coarse_ref, notes_ref[8:, :1], high_ref, low_ref, pl.ds(0, half), image_out)
    image_out[pl.ds(pair_ref.shape[0] // 2 * half // 128, 8), :] = notes_ref[:8, :]


def start_kernel(own_ref, other_ref, front_out, back_out):
    count, half = own_ref.shape
    tiles = half // 128
    for tile in range(tiles):
        out = front_out if tile < tiles // 2 else back_out
        span = pl.ds(tile * 128, 128)
        out[pl.ds(tile % (tiles // 2) * count, count), :] = own_ref[:, span] + other_ref[:, span]


def join_kernel(own_ref, other_ref, front_out, back_out):
    middle, end = back_out.shape[0], 2 * back_out.shape[0]
    front_out[:middle, :] = own_ref[:middle, :] + other_ref[:middle, :]
    front_out[middle:, :] = own_ref[end:, :] + other_ref[end:, :]
    back_out[...] = own_ref[middle:end, :] + other_ref[middle:end, :]


def add_kernel(one_ref, other_ref, sum_ref):
    sum_ref[...] = one_ref[...] + other_ref[...]


def places(targets_ref, front, back):
    count, half = targets_ref.shape
    tiles = half // 128
    for tile in range(tiles):
        refs = front if tile < tiles // 2 else back
        yield pl.ds(tile * 128, 128), refs, pl.ds(tile % (tiles // 2) * count, count)


def open_kernel(front, front_last, back, back_last, targets_ref, clipped_out, predicted_out):
    for span, (one, other), rows in places(targets_ref, (front, front_last), (back, back_last)):
        predicted = one[rows, :] + other[rows, :]
        predicted_out[:, span] = predicted
        clipped_out[:, span] = jnp.clip(predicted - targets_ref[:, span], -huber_cap, huber_cap)


def inverse_of(entries, front, front_last, back):
    end = pl.ds(back.shape[0], 8)
    total = jnp.sum(front[end, :] + front_last[end, :], axis=(0, 1), keepdims=True)
    return 1.0 / jnp.sqrt(total / entries + epsilon)


def step_kernel(entries, front, front_last, back, back_last, targets_ref, predicted_ref, *refs):
    tracked_ref = refs[0] if len(refs) == 5 else None
    clipped_out, predicted_out, inverse_out, tracked_out = refs[-4:]
    inverse = inverse_of(entries, front, front_last, back)
    inverse_out[...] = jnp.broadcast_to(inverse, (8, 128))
    for span, (one, other), rows in places(targets_ref, (front, front_last), (back, back_last)):
        tracked = (one[rows, :] + other[rows, :]) * inverse
        if tracked_ref is not None:
            tracked = momentum * tracked_ref[:, span] + tracked
        predicted = predicted_ref[:, span] - step_rate * tracked
        tracked_out[:, span] = tracked
        predicted_out[:, span] = predicted
        clipped_out[:, span] = jnp.clip(predicted - targets_ref[:, span], -huber_cap, huber_cap)


def sum_kernel(weights, *refs):
    total = jnp.zeros_like(refs[-1])
    for weight, grad_ref, inverse_ref in zip(weights, refs[:-1:2], refs[1:-1:2]):
        total = total + (weight * inverse_ref[0:1, 0:1]) * grad_ref[...]
    refs[-1][...] = total


def close_kernel(entries, weight, front, front_last, back, back_last, targets_ref, predicted_ref, tracked_ref, *refs):
    coeffs_ref, taken_ref, other_taken, grad_ref, other_grad, predicted_out, coeffs_out = refs
    inverse = inverse_of(entries, front, front_last, back)
    for span, (one, other), rows in places(targets_ref, (front, front_last), (back, back_last)):
        tracked = momentum * tracked_ref[:, span] + (one[rows, :] + other[rows, :]) * inverse
        predicted_out[:, span] = predicted_ref[:, span] - step_rate * tracked
    width = taken_ref.shape[1]
    core = lax.axis_index("paths")
    factor = weight * inverse
    for start, taken, grad in ((core, taken_ref, grad_ref), (1 - core, other_taken, other_grad)):
        span = pl.ds(pl.multiple_of(start * width, width), width)
        coeffs_out[:, span] = coeffs_ref[:, span] - (taken[...] + factor * grad[...])


def vmem(count):
    return [pl.BlockSpec(memory_space=pltpu.VMEM)] * count


def held(array):
    return pltpu.with_memory_space_constraint(array, pltpu.VMEM)


def call(kernel, name, arguments, shapes, specs=None, scratch=(), megabytes=4, aliases={}):
    shapes = tuple(shape if not isinstance(shape, tuple) else jax.ShapeDtypeStruct(shape, f32) for shape in shapes)
    return pl.pallas_call(
        kernel,
        out_shape=shapes,
        in_specs=specs or vmem(len(arguments)),
        out_specs=tuple(vmem(len(shapes))),
        scratch_shapes=scratch,
        compiler_params=pltpu.CompilerParams(vmem_limit_bytes=megabytes * 2**20),
        input_output_aliases=aliases,
        name=name,
    )(*arguments)


def shards(sizes, factors, frequency, phases, amplitude, targets, coeffs_init):
    cores, chips = sizes["paths"], sizes["feats"]
    half, risks = factors.shape
    width = frequency.shape[1] // cores
    count = targets.shape[0]
    paths = half * cores
    entries = count * width * cores * chips
    hops = [1 << bit for bit in range(chips.bit_length() - 1)]

    def swap(array):
        return lax.ppermute(array, "paths", [(0, 1), (1, 0)])

    def add(one, other):
        return call(add_kernel, "add", (one, other), (one.shape,))[0]

    def all_chips(front, back):
        orders = hops, hops[1::-1] + hops[2:]
        sums = [front, back]
        for step in range(len(hops)):
            lasts = [
                lax.ppermute(array, "feats", [(chip, chip ^ order[step]) for chip in range(chips)])
                for array, order in zip(sums, orders)
            ]
            if step < len(hops) - 1:
                sums = [add(array, last) for array, last in zip(sums, lasts)]
        return sums[0], lasts[0], sums[1], lasts[1]

    small, wide, row = (count, half), (count, width), (1, width)
    extent = count * half // 128
    middle = extent // 2
    features = pltpu.VMEM((paths, width), bf16), pltpu.VMEM((paths, width), f8)
    blanks = [
        pl.pallas_call(
            lambda out: None,
            out_shape=feature,
            out_specs=vmem(1)[0],
            compiler_params=pltpu.CompilerParams(vmem_limit_bytes=2**20),
            name=name,
        )()
        for name, feature in zip(("blank_high", "blank_low"), features)
    ]
    deep, cols = 2 * risks, divisor(width, 1024)
    own_factors, freq, start, amp = call(
        prepare_kernel,
        "prepare",
        [
            pltpu.with_memory_space_constraint(array, pltpu.HBM)
            for array in (factors, frequency, phases[None], amplitude[None], coeffs_init)
        ],
        (
            jax.ShapeDtypeStruct((half, deep), bf16),
            jax.ShapeDtypeStruct((deep, width), bf16),
            jax.ShapeDtypeStruct((2 * count, width), bf16),
            row,
        ),
        [pl.BlockSpec(memory_space=pltpu.HBM)] * 5,
        [
            pltpu.VMEM(factors.shape, factors.dtype),
            pltpu.VMEM((width // cols, risks, cols), frequency.dtype),
            pltpu.VMEM(row, phases.dtype),
            pltpu.VMEM(row, f32),
            pltpu.VMEM(wide, f32),
            pltpu.SemaphoreType.DMA((4,)),
            pltpu.SemaphoreType.DMA((width // cols,)),
        ],
        12,
    )
    image_own, image_other, high, low = call(
        build_kernel,
        "build",
        (own_factors, swap(factors), freq, start, held(blanks[0]), held(blanks[1])),
        (small, small, *features),
        None,
        [pltpu.VMEM((half, deep), bf16)],
        GRANT,
        {4: 2, 5: 3},
    )
    sums = all_chips(*call(start_kernel, "start", (image_own, swap(image_other)), ((middle, 128), (middle, 128))))
    clipped, predicted = call(open_kernel, "open", (*sums, targets), (small, small))
    weights = [step_rate * sum(momentum**later for later in range(ITERS - turn)) for turn in range(ITERS)]
    tracked = ()
    grads, inverses = [], []
    for turn in range(ITERS):
        partial = call(own_kernel, "own", (clipped, held(high), held(low)), (wide,), None, (), GRANT)[0]
        pieces = jax.ShapeDtypeStruct((2 * count, width), bf16), jax.ShapeDtypeStruct(wide, f8)
        grad, pair, coarse, image_other, notes = call(
            rest_kernel,
            "rest",
            (swap(clipped), held(high), held(low), partial, amp),
            (wide, *pieces, (extent + 8, 128), (count + 8, 128)),
            None,
            (),
            GRANT,
        )
        image_own = call(
            image_kernel, "image", (pair, coarse, notes, held(high), held(low)), ((extent + 8, 128),), None, (), GRANT
        )[0]
        halves = call(join_kernel, "join", (image_own, swap(image_other)), ((middle + 8, 128), (middle, 128)))
        grads.append(grad)
        if turn == ITERS - 1:
            break
        clipped, predicted, inverse, *tracked = call(
            functools.partial(step_kernel, entries),
            "step",
            (*all_chips(*halves), targets, predicted, *tracked),
            (small, small, (8, 128), small),
        )
        inverses.append(inverse)
    before = [array for pair in zip(grads, inverses) for array in pair]
    taken = call(functools.partial(sum_kernel, weights[:-1]), "sum", before, (wide,))[0]
    predicted, coeffs = call(
        functools.partial(close_kernel, entries, weights[-1]),
        "close",
        (*all_chips(*halves), targets, predicted, *tracked, coeffs_init, taken, swap(taken), grad, swap(grad)),
        (small, (count, width * cores)),
        None,
        (),
        8,
    )
    return (coeffs, predicted)


def solution(mesh):
    return jax.shard_map(
        functools.partial(shards, dict(mesh.shape)),
        mesh=mesh,
        in_specs=(
            P(("groups", "paths"), None),
            P(None, "feats"),
            P("feats"),
            P("feats"),
            P(None, ("groups", "paths")),
            P(None, ("groups", "feats")),
        ),
        out_specs=(P(None, ("groups", "feats")), P(None, ("groups", "paths"))),
        check_vma=False,
    )
```

```python
import functools
import math

import jax
import jax.numpy as jnp
import numpy as np
from jax import lax
from jax.experimental import pallas as pl
from jax.experimental.pallas import tpu as pltpu
from jax.sharding import PartitionSpec as P

ITERS = 3

huber_cap = 1.0
step_rate = 0.2
momentum = 0.9
epsilon = 1e-06

f32 = jnp.float32
bf16 = jnp.bfloat16
f8 = jnp.float8_e4m3fn
NN = (((1,), (0,)), ((), ()))
NT = (((1,), (1,)), ((), ()))
TURN = 0.0025 / (2.0 * math.pi)


def fit_half_angle():
    rest = np.cos(np.linspace(0, np.pi, 4001)) * 0.5
    target = np.cos(np.pi * rest)
    basis = np.stack([rest ** (2 * i) for i in range(4)], 1)
    weight = np.abs(target) + 1e-3
    return np.linalg.lstsq(basis * weight[:, None], target * weight, rcond=None)[0]


HALF = fit_half_angle()
TOP = float(2.0 * HALF[-1] ** 2)
SERIES = [float(term / HALF[-1]) for term in HALF]
LOW = 2.0**15
CLIP = 256.0
GRANT = 20


def split(values):
    high = values.astype(bf16)
    return high, (values - high.astype(f32)).astype(bf16)


def cosine(turns):
    rest = turns - jnp.round(turns)
    square = rest * rest
    series = square + SERIES[2]
    series = series * square + SERIES[1]
    series = series * square + SERIES[0]
    return series * series - 1.0 / TOP


def divisor(size, most):
    while size % most:
        most //= 2
    return most


def padded(factors, width):
    rows, risks = factors.shape
    ones = (lax.broadcasted_iota(jnp.int32, (rows, width - risks), 1) < 3).astype(f32)
    return jnp.concatenate([factors.astype(f32).astype(bf16), ones.astype(bf16)], 1)


def prepare_kernel(
    own_ref, freq_ref, phase_ref, amp_ref, coeffs_ref, factor_out, freq_out, start_out, amp_out,
    own_buf, freq_buf, phase_buf, amp_buf, coeffs_buf, whole_sem, freq_sem,
):
    risks = own_ref.shape[1]
    count = coeffs_ref.shape[0]
    steps, _, cols = freq_buf.shape
    extra = freq_out.shape[0] - risks
    first = lax.axis_index("paths") * cols * steps

    def fetch(index):
        source = pl.ds(pl.multiple_of(first + index * cols, cols), cols)
        return pltpu.make_async_copy(freq_ref.at[:, source], freq_buf.at[index], freq_sem.at[index])

    mine = pl.ds(pl.multiple_of(first, cols), cols * steps)
    wholes = [
        pltpu.make_async_copy(source, target, whole_sem.at[number])
        for number, (source, target) in enumerate(
            (
                (phase_ref.at[:, mine], phase_buf),
                (amp_ref.at[:, mine], amp_buf),
                (coeffs_ref.at[:, mine], coeffs_buf),
                (own_ref, own_buf),
            )
        )
    ]
    for copy in wholes:
        copy.start()
    for index in range(steps):
        fetch(index).start()
    for copy in wholes:
        copy.wait()
    factor_out[...] = padded(own_buf[...], factor_out.shape[1])
    row = lax.broadcasted_iota(jnp.int32, (extra, cols), 0)
    for index in range(steps):
        span = pl.ds(index * cols, cols)
        phase = phase_buf[:, span].astype(f32) * (1.0 / (1024.0 * TURN))
        piece_high = phase.astype(bf16).astype(f32)
        piece_middle = (phase - piece_high).astype(bf16).astype(f32)
        piece_low = phase - piece_high - piece_middle
        pieces = jnp.where(row == 0, piece_high, jnp.where(row == 1, piece_middle, jnp.where(row == 2, piece_low, 0.0)))
        freq_out[risks:, span] = pieces.astype(bf16)
        amp = amp_buf[:, span] * TOP
        amp_out[:, span] = amp
        start_high, start_low = split(coeffs_buf[:, span] * amp)
        start_out[:count, span] = start_high
        start_out[count:, span] = start_low
    for index in range(steps):
        fetch(index).wait()
        freq_out[:risks, pl.ds(index * cols, cols)] = freq_buf[index].astype(f32).astype(bf16)


def build_kernel(
    own_ref, other_ref, freq_ref, start_ref, blank_high, blank_low, image_own, image_other, high_ref, low_ref, other_buf
):
    paths, width = high_ref.shape
    half = paths // 2
    cols = divisor(width, 1024)
    rows = divisor(half, 512)
    count = start_ref.shape[0] // 2
    other_buf[...] = padded(other_ref[...], other_buf.shape[1])

    image_own[...] = jnp.zeros_like(image_own)
    image_other[...] = jnp.zeros_like(image_other)

    def block(index, carry):
        span = pl.ds(pl.multiple_of(index * cols, cols), cols)
        freq, start = freq_ref[:, span], start_ref[:, span]

        def sums_of(part):
            factor_ref = own_ref if part * rows < half else other_buf
            factors = factor_ref[pl.ds(part * rows % half, rows), :]
            return lax.dot_general(factors, freq, NN, preferred_element_type=f32)

        def add_image(part, high, low):
            main = lax.dot_general(start, high, NT, preferred_element_type=f32)
            rest = lax.dot_general(low, start[:count], NT, preferred_element_type=f32)
            image_ref = image_own if part * rows < half else image_other
            image_ref[:, pl.ds(part * rows % half, rows)] += main[:count] + main[count:] + rest.T

        parts = paths // rows
        summed = sums_of(0)
        before = None
        for part in range(parts):
            summed_after = sums_of(part + 1) if part + 1 < parts else None
            place = pl.ds(part * rows, rows)
            values = cosine(summed * TURN)
            high = values.astype(bf16)
            rest = values - high.astype(f32)
            high_ref[place, span] = high
            low_ref[place, span] = (rest * LOW).astype(f8)
            if before is not None:
                add_image(*before)
            before = part, high, rest.astype(bf16)
            summed = summed_after
        add_image(*before)
        return carry

    lax.fori_loop(0, width // cols, block, 0)


def gradient_of(clipped, high_ref, low_ref, place, span):
    count = clipped.shape[0]
    pair = jnp.concatenate(split(clipped), 0)
    main = lax.dot_general(pair, high_ref[place, span], NN, preferred_element_type=f32)
    coarse = (clipped * CLIP).astype(f8)
    rest = lax.dot_general(coarse, low_ref[place, span], NN, preferred_element_type=f32)
    return main[:count] + main[count:] + rest * (1.0 / (CLIP * LOW))


def image_of(pair_ref, coarse_ref, level, high_ref, low_ref, place, image_ref):
    count = pair_ref.shape[0] // 2
    main = lax.dot_general(pair_ref[...], high_ref[place, :], NT, preferred_element_type=f32)
    rest = lax.dot_general(coarse_ref[...], low_ref[place, :], NT, preferred_element_type=f32)
    image = main[:count] + main[count:] + rest * (level * (1.0 / LOW))
    for tile in range(image.shape[1] // 128):
        image_ref[pl.ds(tile * count, count), :] = image[:, tile * 128 : tile * 128 + 128]


def own_kernel(clipped_ref, high_ref, low_ref, partial_out):
    paths, width = high_ref.shape
    cols = divisor(width, 1024)
    for index in range(width // cols):
        span = pl.ds(index * cols, cols)
        partial_out[:, span] = gradient_of(clipped_ref[...], high_ref, low_ref, pl.ds(0, paths // 2), span)


def rest_kernel(
    clipped_ref, high_ref, low_ref, partial_ref, amp_ref, grad_out, pair_out, coarse_out, image_out, notes_out
):
    paths, width = high_ref.shape
    half = paths // 2
    count = clipped_ref.shape[0]
    cols = divisor(width, 1024)
    squares = jnp.zeros((8, 128), f32)
    largest = jnp.zeros((count, 128), f32)
    for index in range(width // cols):
        span = pl.ds(index * cols, cols)
        share = gradient_of(clipped_ref[...], high_ref, low_ref, pl.ds(half, half), span)
        amp = amp_ref[:, span]
        grad = (partial_ref[:, span] + share) * amp
        grad_out[:, span] = grad
        pushed = grad * amp
        high, low = split(pushed)
        pair_out[:count, span] = high
        pair_out[count:, span] = low
        for lane in range(0, cols, 128):
            largest = jnp.maximum(largest, jnp.abs(pushed[:, lane : lane + 128]))
            for row in range(0, count, 8):
                tile = grad[row : row + 8, lane : lane + 128]
                squares = squares + tile * tile
    level = jnp.maximum(jnp.max(largest, axis=1, keepdims=True), 1e-30) * (1.0 / 240.0)
    for index in range(width // cols):
        span = pl.ds(index * cols, cols)
        coarse_out[:, span] = (pair_out[:count, span].astype(f32) * (1.0 / level)).astype(f8)
    image_of(pair_out, coarse_out, level, high_ref, low_ref, pl.ds(half, half), image_out)
    image_out[pl.ds(count * half // 128, 8), :] = squares
    notes_out[:8, :] = squares
    notes_out[8:, :] = jnp.broadcast_to(level, (count, 128))


def image_kernel(pair_ref, coarse_ref, notes_ref, high_ref, low_ref, image_out):
    half = high_ref.shape[0] // 2
    image_of(pair_ref, coarse_ref, notes_ref[8:, :1], high_ref, low_ref, pl.ds(0, half), image_out)
    image_out[pl.ds(pair_ref.shape[0] // 2 * half // 128, 8), :] = notes_ref[:8, :]


def start_kernel(own_ref, other_ref, front_out, back_out):
    count, half = own_ref.shape
    tiles = half // 128
    for tile in range(tiles):
        out = front_out if tile < tiles // 2 else back_out
        span = pl.ds(tile * 128, 128)
        out[pl.ds(tile % (tiles // 2) * count, count), :] = own_ref[:, span] + other_ref[:, span]


def join_kernel(own_ref, other_ref, front_out, back_out):
    middle, end = back_out.shape[0], 2 * back_out.shape[0]
    front_out[:middle, :] = own_ref[:middle, :] + other_ref[:middle, :]
    front_out[middle:, :] = own_ref[end:, :] + other_ref[end:, :]
    back_out[...] = own_ref[middle:end, :] + other_ref[middle:end, :]


def add_kernel(one_ref, other_ref, sum_ref):
    sum_ref[...] = one_ref[...] + other_ref[...]


def places(targets_ref, front, back):
    count, half = targets_ref.shape
    tiles = half // 128
    for tile in range(tiles):
        refs = front if tile < tiles // 2 else back
        yield pl.ds(tile * 128, 128), refs, pl.ds(tile % (tiles // 2) * count, count)


def open_kernel(front, front_last, back, back_last, targets_ref, clipped_out, predicted_out):
    for span, (one, other), rows in places(targets_ref, (front, front_last), (back, back_last)):
        predicted = one[rows, :] + other[rows, :]
        predicted_out[:, span] = predicted
        clipped_out[:, span] = jnp.clip(predicted - targets_ref[:, span], -huber_cap, huber_cap)


def inverse_of(entries, front, front_last, back):
    end = pl.ds(back.shape[0], 8)
    total = jnp.sum(front[end, :] + front_last[end, :], axis=(0, 1), keepdims=True)
    return 1.0 / jnp.sqrt(total / entries + epsilon)


def step_kernel(entries, front, front_last, back, back_last, targets_ref, predicted_ref, *refs):
    tracked_ref = refs[0] if len(refs) == 5 else None
    clipped_out, predicted_out, inverse_out, tracked_out = refs[-4:]
    inverse = inverse_of(entries, front, front_last, back)
    inverse_out[...] = jnp.broadcast_to(inverse, (8, 128))
    for span, (one, other), rows in places(targets_ref, (front, front_last), (back, back_last)):
        tracked = (one[rows, :] + other[rows, :]) * inverse
        if tracked_ref is not None:
            tracked = momentum * tracked_ref[:, span] + tracked
        predicted = predicted_ref[:, span] - step_rate * tracked
        tracked_out[:, span] = tracked
        predicted_out[:, span] = predicted
        clipped_out[:, span] = jnp.clip(predicted - targets_ref[:, span], -huber_cap, huber_cap)


def sum_kernel(weights, *refs):
    total = jnp.zeros_like(refs[-1])
    for weight, grad_ref, inverse_ref in zip(weights, refs[:-1:2], refs[1:-1:2]):
        total = total + (weight * inverse_ref[0:1, 0:1]) * grad_ref[...]
    refs[-1][...] = total


def close_kernel(entries, weight, front, front_last, back, back_last, targets_ref, predicted_ref, tracked_ref, *refs):
    coeffs_ref, taken_ref, other_taken, grad_ref, other_grad, predicted_out, coeffs_out = refs
    inverse = inverse_of(entries, front, front_last, back)
    for span, (one, other), rows in places(targets_ref, (front, front_last), (back, back_last)):
        tracked = momentum * tracked_ref[:, span] + (one[rows, :] + other[rows, :]) * inverse
        predicted_out[:, span] = predicted_ref[:, span] - step_rate * tracked
    width = taken_ref.shape[1]
    core = lax.axis_index("paths")
    factor = weight * inverse
    for start, taken, grad in ((core, taken_ref, grad_ref), (1 - core, other_taken, other_grad)):
        span = pl.ds(pl.multiple_of(start * width, width), width)
        coeffs_out[:, span] = coeffs_ref[:, span] - (taken[...] + factor * grad[...])


def vmem(count):
    return [pl.BlockSpec(memory_space=pltpu.VMEM)] * count


def held(array):
    return pltpu.with_memory_space_constraint(array, pltpu.VMEM)


def call(kernel, name, arguments, shapes, specs=None, scratch=(), megabytes=4, aliases={}):
    shapes = tuple(shape if not isinstance(shape, tuple) else jax.ShapeDtypeStruct(shape, f32) for shape in shapes)
    return pl.pallas_call(
        kernel,
        out_shape=shapes,
        in_specs=specs or vmem(len(arguments)),
        out_specs=tuple(vmem(len(shapes))),
        scratch_shapes=scratch,
        compiler_params=pltpu.CompilerParams(vmem_limit_bytes=megabytes * 2**20),
        input_output_aliases=aliases,
        name=name,
    )(*arguments)


def shards(sizes, factors, frequency, phases, amplitude, targets, coeffs_init):
    cores, chips = sizes["paths"], sizes["feats"]
    half, risks = factors.shape
    width = frequency.shape[1] // cores
    count = targets.shape[0]
    paths = half * cores
    entries = count * width * cores * chips
    hops = [1 << bit for bit in range(chips.bit_length() - 1)]

    def swap(array):
        return lax.ppermute(array, "paths", [(0, 1), (1, 0)])

    def add(one, other):
        return call(add_kernel, "add", (one, other), (one.shape,))[0]

    def all_chips(front, back):
        orders = hops, hops[1::-1] + hops[2:]
        sums = [front, back]
        for step in range(len(hops)):
            lasts = [
                lax.ppermute(array, "feats", [(chip, chip ^ order[step]) for chip in range(chips)])
                for array, order in zip(sums, orders)
            ]
            if step < len(hops) - 1:
                sums = [add(array, last) for array, last in zip(sums, lasts)]
        return sums[0], lasts[0], sums[1], lasts[1]

    small, wide, row = (count, half), (count, width), (1, width)
    extent = count * half // 128
    middle = extent // 2
    features = pltpu.VMEM((paths, width), bf16), pltpu.VMEM((paths, width), f8)
    blanks = [
        pl.pallas_call(
            lambda out: None,
            out_shape=feature,
            out_specs=vmem(1)[0],
            compiler_params=pltpu.CompilerParams(vmem_limit_bytes=2**20),
            name=name,
        )()
        for name, feature in zip(("blank_high", "blank_low"), features)
    ]
    deep, cols = 2 * risks, divisor(width, 1024)
    own_factors, freq, start, amp = call(
        prepare_kernel,
        "prepare",
        [
            pltpu.with_memory_space_constraint(array, pltpu.HBM)
            for array in (factors, frequency, phases[None], amplitude[None], coeffs_init)
        ],
        (
            jax.ShapeDtypeStruct((half, deep), bf16),
            jax.ShapeDtypeStruct((deep, width), bf16),
            jax.ShapeDtypeStruct((2 * count, width), bf16),
            row,
        ),
        [pl.BlockSpec(memory_space=pltpu.HBM)] * 5,
        [
            pltpu.VMEM(factors.shape, factors.dtype),
            pltpu.VMEM((width // cols, risks, cols), frequency.dtype),
            pltpu.VMEM(row, phases.dtype),
            pltpu.VMEM(row, f32),
            pltpu.VMEM(wide, f32),
            pltpu.SemaphoreType.DMA((4,)),
            pltpu.SemaphoreType.DMA((width // cols,)),
        ],
        12,
    )
    image_own, image_other, high, low = call(
        build_kernel,
        "build",
        (own_factors, swap(factors), freq, start, held(blanks[0]), held(blanks[1])),
        (small, small, *features),
        None,
        [pltpu.VMEM((half, deep), bf16)],
        GRANT,
        {4: 2, 5: 3},
    )
    sums = all_chips(*call(start_kernel, "start", (image_own, swap(image_other)), ((middle, 128), (middle, 128))))
    clipped, predicted = call(open_kernel, "open", (*sums, targets), (small, small))
    weights = [step_rate * sum(momentum**later for later in range(ITERS - turn)) for turn in range(ITERS)]
    tracked = ()
    grads, inverses = [], []
    for turn in range(ITERS):
        partial = call(own_kernel, "own", (clipped, held(high), held(low)), (wide,), None, (), GRANT)[0]
        pieces = jax.ShapeDtypeStruct((2 * count, width), bf16), jax.ShapeDtypeStruct(wide, f8)
        grad, pair, coarse, image_other, notes = call(
            rest_kernel,
            "rest",
            (swap(clipped), held(high), held(low), partial, amp),
            (wide, *pieces, (extent + 8, 128), (count + 8, 128)),
            None,
            (),
            GRANT,
        )
        image_own = call(
            image_kernel, "image", (pair, coarse, notes, held(high), held(low)), ((extent + 8, 128),), None, (), GRANT
        )[0]
        halves = call(join_kernel, "join", (image_own, swap(image_other)), ((middle + 8, 128), (middle, 128)))
        grads.append(grad)
        if turn == ITERS - 1:
            break
        clipped, predicted, inverse, *tracked = call(
            functools.partial(step_kernel, entries),
            "step",
            (*all_chips(*halves), targets, predicted, *tracked),
            (small, small, (8, 128), small),
        )
        inverses.append(inverse)
    before = [array for pair in zip(grads, inverses) for array in pair]
    taken = call(functools.partial(sum_kernel, weights[:-1]), "sum", before, (wide,))[0]
    predicted, coeffs = call(
        functools.partial(close_kernel, entries, weights[-1]),
        "close",
        (*all_chips(*halves), targets, predicted, *tracked, coeffs_init, taken, swap(taken), grad, swap(grad)),
        (small, (count, width * cores)),
        None,
        (),
        8,
    )
    return (coeffs, predicted)


def solution(mesh):
    return jax.shard_map(
        functools.partial(shards, dict(mesh.shape)),
        mesh=mesh,
        in_specs=(
            P(("groups", "paths"), None),
            P(None, "feats"),
            P("feats"),
            P("feats"),
            P(None, ("groups", "paths")),
            P(None, ("groups", "feats")),
        ),
        out_specs=(P(None, ("groups", "feats")), P(None, ("groups", "paths"))),
        check_vma=False,
    )
```

```python
import functools
import math

import jax
import jax.numpy as jnp
import numpy as np
from jax import lax
from jax.experimental import pallas as pl
from jax.experimental.pallas import tpu as pltpu
from jax.sharding import PartitionSpec as P

ITERS = 3

huber_cap = 1.0
step_rate = 0.2
momentum = 0.9
epsilon = 1e-06

f32 = jnp.float32
bf16 = jnp.bfloat16
f8 = jnp.float8_e4m3fn
NN = (((1,), (0,)), ((), ()))
NT = (((1,), (1,)), ((), ()))
TURN = 0.0025 / (2.0 * math.pi)


def fit_half_angle():
    rest = np.cos(np.linspace(0, np.pi, 4001)) * 0.5
    target = np.cos(np.pi * rest)
    basis = np.stack([rest ** (2 * i) for i in range(4)], 1)
    weight = np.abs(target) + 1e-3
    return np.linalg.lstsq(basis * weight[:, None], target * weight, rcond=None)[0]


HALF = fit_half_angle()
TOP = float(2.0 * HALF[-1] ** 2)
SERIES = [float(term / HALF[-1]) for term in HALF]
LOW = 2.0**15
CLIP = 256.0
GRANT = 20


def split(values):
    high = values.astype(bf16)
    return high, (values - high.astype(f32)).astype(bf16)


def cosine(turns):
    rest = turns - jnp.round(turns)
    square = rest * rest
    series = square + SERIES[2]
    series = series * square + SERIES[1]
    series = series * square + SERIES[0]
    return series * series - 1.0 / TOP


def divisor(size, most):
    while size % most:
        most //= 2
    return most


def padded(factors, width):
    rows, risks = factors.shape
    ones = (lax.broadcasted_iota(jnp.int32, (rows, width - risks), 1) < 3).astype(f32)
    return jnp.concatenate([factors.astype(f32).astype(bf16), ones.astype(bf16)], 1)


def prepare_kernel(
    own_ref, freq_ref, phase_ref, amp_ref, coeffs_ref, factor_out, freq_out, start_out, amp_out,
    own_buf, freq_buf, phase_buf, amp_buf, coeffs_buf, whole_sem, freq_sem,
):
    risks = own_ref.shape[1]
    count = coeffs_ref.shape[0]
    steps, _, cols = freq_buf.shape
    extra = freq_out.shape[0] - risks
    first = lax.axis_index("paths") * cols * steps

    def fetch(index):
        source = pl.ds(pl.multiple_of(first + index * cols, cols), cols)
        return pltpu.make_async_copy(freq_ref.at[:, source], freq_buf.at[index], freq_sem.at[index])

    mine = pl.ds(pl.multiple_of(first, cols), cols * steps)
    wholes = [
        pltpu.make_async_copy(source, target, whole_sem.at[number])
        for number, (source, target) in enumerate(
            (
                (phase_ref.at[:, mine], phase_buf),
                (amp_ref.at[:, mine], amp_buf),
                (coeffs_ref.at[:, mine], coeffs_buf),
                (own_ref, own_buf),
            )
        )
    ]
    for copy in wholes:
        copy.start()
    for index in range(steps):
        fetch(index).start()
    for copy in wholes:
        copy.wait()
    factor_out[...] = padded(own_buf[...], factor_out.shape[1])
    row = lax.broadcasted_iota(jnp.int32, (extra, cols), 0)
    for index in range(steps):
        span = pl.ds(index * cols, cols)
        phase = phase_buf[:, span].astype(f32) * (1.0 / (1024.0 * TURN))
        piece_high = phase.astype(bf16).astype(f32)
        piece_middle = (phase - piece_high).astype(bf16).astype(f32)
        piece_low = phase - piece_high - piece_middle
        pieces = jnp.where(row == 0, piece_high, jnp.where(row == 1, piece_middle, jnp.where(row == 2, piece_low, 0.0)))
        freq_out[risks:, span] = pieces.astype(bf16)
        amp = amp_buf[:, span] * TOP
        amp_out[:, span] = amp
        start_high, start_low = split(coeffs_buf[:, span] * amp)
        start_out[:count, span] = start_high
        start_out[count:, span] = start_low
    for index in range(steps):
        fetch(index).wait()
        freq_out[:risks, pl.ds(index * cols, cols)] = freq_buf[index].astype(f32).astype(bf16)


def build_kernel(
    own_ref, other_ref, freq_ref, start_ref, blank_high, blank_low, image_own, image_other, high_ref, low_ref, other_buf
):
    paths, width = high_ref.shape
    half = paths // 2
    cols = divisor(width, 1024)
    rows = divisor(half, 512)
    count = start_ref.shape[0] // 2
    other_buf[...] = padded(other_ref[...], other_buf.shape[1])

    image_own[...] = jnp.zeros_like(image_own)
    image_other[...] = jnp.zeros_like(image_other)

    def block(index, carry):
        span = pl.ds(pl.multiple_of(index * cols, cols), cols)
        freq, start = freq_ref[:, span], start_ref[:, span]

        def sums_of(part):
            factor_ref = own_ref if part * rows < half else other_buf
            factors = factor_ref[pl.ds(part * rows % half, rows), :]
            return lax.dot_general(factors, freq, NN, preferred_element_type=f32)

        def add_image(part, high, low):
            main = lax.dot_general(start, high, NT, preferred_element_type=f32)
            rest = lax.dot_general(low, start[:count], NT, preferred_element_type=f32)
            image_ref = image_own if part * rows < half else image_other
            image_ref[:, pl.ds(part * rows % half, rows)] += main[:count] + main[count:] + rest.T

        parts = paths // rows
        summed = sums_of(0)
        before = None
        for part in range(parts):
            summed_after = sums_of(part + 1) if part + 1 < parts else None
            place = pl.ds(part * rows, rows)
            values = cosine(summed * TURN)
            high = values.astype(bf16)
            rest = values - high.astype(f32)
            high_ref[place, span] = high
            low_ref[place, span] = (rest * LOW).astype(f8)
            if before is not None:
                add_image(*before)
            before = part, high, rest.astype(bf16)
            summed = summed_after
        add_image(*before)
        return carry

    lax.fori_loop(0, width // cols, block, 0)


def gradient_of(clipped, high_ref, low_ref, place, span):
    count = clipped.shape[0]
    pair = jnp.concatenate(split(clipped), 0)
    main = lax.dot_general(pair, high_ref[place, span], NN, preferred_element_type=f32)
    coarse = (clipped * CLIP).astype(f8)
    rest = lax.dot_general(coarse, low_ref[place, span], NN, preferred_element_type=f32)
    return main[:count] + main[count:] + rest * (1.0 / (CLIP * LOW))


def image_of(pair_ref, coarse_ref, level, high_ref, low_ref, start, image_ref):
    count, half = pair_ref.shape[0] // 2, high_ref.shape[0] // 2
    rows = divisor(half, 512)
    for first in range(0, half, rows):
        place = pl.ds(start + first, rows)
        main = lax.dot_general(high_ref[place, :], pair_ref[...], NT, preferred_element_type=f32).T
        rest = lax.dot_general(coarse_ref[...], low_ref[place, :], NT, preferred_element_type=f32)
        image = main[:count] + main[count:] + rest * (level * (1.0 / LOW))
        for lane in range(0, rows, 128):
            image_ref[pl.ds((first + lane) // 128 * count, count), :] = image[:, lane : lane + 128]


def own_kernel(clipped_ref, high_ref, low_ref, partial_out):
    paths, width = high_ref.shape
    cols = divisor(width, 1024)
    for index in range(width // cols):
        span = pl.ds(index * cols, cols)
        partial_out[:, span] = gradient_of(clipped_ref[...], high_ref, low_ref, pl.ds(0, paths // 2), span)


def rest_kernel(
    clipped_ref, high_ref, low_ref, partial_ref, amp_ref, grad_out, pair_out, coarse_out, image_out, notes_out
):
    paths, width = high_ref.shape
    half = paths // 2
    count = clipped_ref.shape[0]
    cols = divisor(width, 1024)
    squares = jnp.zeros((8, 128), f32)
    largest = jnp.zeros((count, 128), f32)
    for index in range(width // cols):
        span = pl.ds(index * cols, cols)
        share = gradient_of(clipped_ref[...], high_ref, low_ref, pl.ds(half, half), span)
        amp = amp_ref[:, span]
        grad = (partial_ref[:, span] + share) * amp
        grad_out[:, span] = grad
        pushed = grad * amp
        high, low = split(pushed)
        pair_out[:count, span] = high
        pair_out[count:, span] = low
        for lane in range(0, cols, 128):
            largest = jnp.maximum(largest, jnp.abs(pushed[:, lane : lane + 128]))
            for row in range(0, count, 8):
                tile = grad[row : row + 8, lane : lane + 128]
                squares = squares + tile * tile
    level = jnp.maximum(jnp.max(largest, axis=1, keepdims=True), 1e-30) * (1.0 / 240.0)
    for index in range(width // cols):
        span = pl.ds(index * cols, cols)
        coarse_out[:, span] = (pair_out[:count, span].astype(f32) * (1.0 / level)).astype(f8)
    image_of(pair_out, coarse_out, level, high_ref, low_ref, half, image_out)
    image_out[pl.ds(count * half // 128, 8), :] = squares
    notes_out[:8, :] = squares
    notes_out[8:, :] = jnp.broadcast_to(level, (count, 128))


def image_kernel(pair_ref, coarse_ref, notes_ref, high_ref, low_ref, image_out):
    half = high_ref.shape[0] // 2
    image_of(pair_ref, coarse_ref, notes_ref[8:, :1], high_ref, low_ref, 0, image_out)
    image_out[pl.ds(pair_ref.shape[0] // 2 * half // 128, 8), :] = notes_ref[:8, :]


def start_kernel(own_ref, other_ref, front_out, back_out):
    count, half = own_ref.shape
    tiles = half // 128
    for tile in range(tiles):
        out = front_out if tile < tiles // 2 else back_out
        span = pl.ds(tile * 128, 128)
        out[pl.ds(tile % (tiles // 2) * count, count), :] = own_ref[:, span] + other_ref[:, span]


def join_kernel(own_ref, other_ref, front_out, back_out):
    middle, end = back_out.shape[0], 2 * back_out.shape[0]
    front_out[:middle, :] = own_ref[:middle, :] + other_ref[:middle, :]
    front_out[middle:, :] = own_ref[end:, :] + other_ref[end:, :]
    back_out[...] = own_ref[middle:end, :] + other_ref[middle:end, :]


def add_kernel(one_ref, other_ref, sum_ref):
    sum_ref[...] = one_ref[...] + other_ref[...]


def places(targets_ref, front, back):
    count, half = targets_ref.shape
    tiles = half // 128
    for tile in range(tiles):
        refs = front if tile < tiles // 2 else back
        yield pl.ds(tile * 128, 128), refs, pl.ds(tile % (tiles // 2) * count, count)


def open_kernel(front, front_last, back, back_last, targets_ref, clipped_out, predicted_out):
    for span, (one, other), rows in places(targets_ref, (front, front_last), (back, back_last)):
        predicted = one[rows, :] + other[rows, :]
        predicted_out[:, span] = predicted
        clipped_out[:, span] = jnp.clip(predicted - targets_ref[:, span], -huber_cap, huber_cap)


def inverse_of(entries, front, front_last, back):
    end = pl.ds(back.shape[0], 8)
    total = jnp.sum(front[end, :] + front_last[end, :], axis=(0, 1), keepdims=True)
    return 1.0 / jnp.sqrt(total / entries + epsilon)


def step_kernel(entries, front, front_last, back, back_last, targets_ref, predicted_ref, *refs):
    tracked_ref = refs[0] if len(refs) == 5 else None
    clipped_out, predicted_out, inverse_out, tracked_out = refs[-4:]
    inverse = inverse_of(entries, front, front_last, back)
    inverse_out[...] = jnp.broadcast_to(inverse, (8, 128))
    for span, (one, other), rows in places(targets_ref, (front, front_last), (back, back_last)):
        tracked = (one[rows, :] + other[rows, :]) * inverse
        if tracked_ref is not None:
            tracked = momentum * tracked_ref[:, span] + tracked
        predicted = predicted_ref[:, span] - step_rate * tracked
        tracked_out[:, span] = tracked
        predicted_out[:, span] = predicted
        clipped_out[:, span] = jnp.clip(predicted - targets_ref[:, span], -huber_cap, huber_cap)


def sum_kernel(weights, *refs):
    total = jnp.zeros_like(refs[-1])
    for weight, grad_ref, inverse_ref in zip(weights, refs[:-1:2], refs[1:-1:2]):
        total = total + (weight * inverse_ref[0:1, 0:1]) * grad_ref[...]
    refs[-1][...] = total


def close_kernel(entries, weight, front, front_last, back, back_last, targets_ref, predicted_ref, tracked_ref, *refs):
    coeffs_ref, taken_ref, other_taken, grad_ref, other_grad, predicted_out, coeffs_out = refs
    inverse = inverse_of(entries, front, front_last, back)
    for span, (one, other), rows in places(targets_ref, (front, front_last), (back, back_last)):
        tracked = momentum * tracked_ref[:, span] + (one[rows, :] + other[rows, :]) * inverse
        predicted_out[:, span] = predicted_ref[:, span] - step_rate * tracked
    width = taken_ref.shape[1]
    core = lax.axis_index("paths")
    factor = weight * inverse
    for start, taken, grad in ((core, taken_ref, grad_ref), (1 - core, other_taken, other_grad)):
        span = pl.ds(pl.multiple_of(start * width, width), width)
        coeffs_out[:, span] = coeffs_ref[:, span] - (taken[...] + factor * grad[...])


def vmem(count):
    return [pl.BlockSpec(memory_space=pltpu.VMEM)] * count


def held(array):
    return pltpu.with_memory_space_constraint(array, pltpu.VMEM)


def call(kernel, name, arguments, shapes, specs=None, scratch=(), megabytes=4, aliases={}):
    shapes = tuple(shape if not isinstance(shape, tuple) else jax.ShapeDtypeStruct(shape, f32) for shape in shapes)
    return pl.pallas_call(
        kernel,
        out_shape=shapes,
        in_specs=specs or vmem(len(arguments)),
        out_specs=tuple(vmem(len(shapes))),
        scratch_shapes=scratch,
        compiler_params=pltpu.CompilerParams(vmem_limit_bytes=megabytes * 2**20),
        input_output_aliases=aliases,
        name=name,
    )(*arguments)


def shards(sizes, factors, frequency, phases, amplitude, targets, coeffs_init):
    cores, chips = sizes["paths"], sizes["feats"]
    half, risks = factors.shape
    width = frequency.shape[1] // cores
    count = targets.shape[0]
    paths = half * cores
    entries = count * width * cores * chips
    hops = [1 << bit for bit in range(chips.bit_length() - 1)]

    def swap(array):
        return lax.ppermute(array, "paths", [(0, 1), (1, 0)])

    def add(one, other):
        return call(add_kernel, "add", (one, other), (one.shape,))[0]

    def all_chips(front, back):
        orders = hops, hops[1::-1] + hops[2:]
        sums = [front, back]
        for step in range(len(hops)):
            lasts = [
                lax.ppermute(array, "feats", [(chip, chip ^ order[step]) for chip in range(chips)])
                for array, order in zip(sums, orders)
            ]
            if step < len(hops) - 1:
                sums = [add(array, last) for array, last in zip(sums, lasts)]
        return sums[0], lasts[0], sums[1], lasts[1]

    small, wide, row = (count, half), (count, width), (1, width)
    extent = count * half // 128
    middle = extent // 2
    features = pltpu.VMEM((paths, width), bf16), pltpu.VMEM((paths, width), f8)
    blanks = [
        pl.pallas_call(
            lambda out: None,
            out_shape=feature,
            out_specs=vmem(1)[0],
            compiler_params=pltpu.CompilerParams(vmem_limit_bytes=2**20),
            name=name,
        )()
        for name, feature in zip(("blank_high", "blank_low"), features)
    ]
    deep, cols = 2 * risks, divisor(width, 1024)
    own_factors, freq, start, amp = call(
        prepare_kernel,
        "prepare",
        [
            pltpu.with_memory_space_constraint(array, pltpu.HBM)
            for array in (factors, frequency, phases[None], amplitude[None], coeffs_init)
        ],
        (
            jax.ShapeDtypeStruct((half, deep), bf16),
            jax.ShapeDtypeStruct((deep, width), bf16),
            jax.ShapeDtypeStruct((2 * count, width), bf16),
            row,
        ),
        [pl.BlockSpec(memory_space=pltpu.HBM)] * 5,
        [
            pltpu.VMEM(factors.shape, factors.dtype),
            pltpu.VMEM((width // cols, risks, cols), frequency.dtype),
            pltpu.VMEM(row, phases.dtype),
            pltpu.VMEM(row, f32),
            pltpu.VMEM(wide, f32),
            pltpu.SemaphoreType.DMA((4,)),
            pltpu.SemaphoreType.DMA((width // cols,)),
        ],
        12,
    )
    image_own, image_other, high, low = call(
        build_kernel,
        "build",
        (own_factors, swap(factors), freq, start, held(blanks[0]), held(blanks[1])),
        (small, small, *features),
        None,
        [pltpu.VMEM((half, deep), bf16)],
        GRANT,
        {4: 2, 5: 3},
    )
    sums = all_chips(*call(start_kernel, "start", (image_own, swap(image_other)), ((middle, 128), (middle, 128))))
    clipped, predicted = call(open_kernel, "open", (*sums, targets), (small, small))
    weights = [step_rate * sum(momentum**later for later in range(ITERS - turn)) for turn in range(ITERS)]
    tracked = ()
    grads, inverses = [], []
    for turn in range(ITERS):
        partial = call(own_kernel, "own", (clipped, held(high), held(low)), (wide,), None, (), GRANT)[0]
        pieces = jax.ShapeDtypeStruct((2 * count, width), bf16), jax.ShapeDtypeStruct(wide, f8)
        grad, pair, coarse, image_other, notes = call(
            rest_kernel,
            "rest",
            (swap(clipped), held(high), held(low), partial, amp),
            (wide, *pieces, (extent + 8, 128), (count + 8, 128)),
            None,
            (),
            GRANT,
        )
        image_own = call(
            image_kernel, "image", (pair, coarse, notes, held(high), held(low)), ((extent + 8, 128),), None, (), GRANT
        )[0]
        halves = call(join_kernel, "join", (image_own, swap(image_other)), ((middle + 8, 128), (middle, 128)))
        grads.append(grad)
        if turn == ITERS - 1:
            break
        clipped, predicted, inverse, *tracked = call(
            functools.partial(step_kernel, entries),
            "step",
            (*all_chips(*halves), targets, predicted, *tracked),
            (small, small, (8, 128), small),
        )
        inverses.append(inverse)
    before = [array for pair in zip(grads, inverses) for array in pair]
    taken = call(functools.partial(sum_kernel, weights[:-1]), "sum", before, (wide,))[0]
    predicted, coeffs = call(
        functools.partial(close_kernel, entries, weights[-1]),
        "close",
        (*all_chips(*halves), targets, predicted, *tracked, coeffs_init, taken, swap(taken), grad, swap(grad)),
        (small, (count, width * cores)),
        None,
        (),
        8,
    )
    return (coeffs, predicted)


def solution(mesh):
    return jax.shard_map(
        functools.partial(shards, dict(mesh.shape)),
        mesh=mesh,
        in_specs=(
            P(("groups", "paths"), None),
            P(None, "feats"),
            P("feats"),
            P("feats"),
            P(None, ("groups", "paths")),
            P(None, ("groups", "feats")),
        ),
        out_specs=(P(None, ("groups", "feats")), P(None, ("groups", "paths"))),
        check_vma=False,
    )
```

```python
import functools
import math

import jax
import jax.numpy as jnp
import numpy as np
from jax import lax
from jax.experimental import pallas as pl
from jax.experimental.pallas import tpu as pltpu
from jax.sharding import PartitionSpec as P

ITERS = 3

huber_cap = 1.0
step_rate = 0.2
momentum = 0.9
epsilon = 1e-06

f32 = jnp.float32
bf16 = jnp.bfloat16
f8 = jnp.float8_e4m3fn
NN = (((1,), (0,)), ((), ()))
NT = (((1,), (1,)), ((), ()))
TURN = 0.0025 / (2.0 * math.pi)


def fit_half_angle():
    rest = np.cos(np.linspace(0, np.pi, 4001)) * 0.5
    target = np.cos(np.pi * rest)
    basis = np.stack([rest ** (2 * i) for i in range(4)], 1)
    weight = np.abs(target) + 1e-3
    return np.linalg.lstsq(basis * weight[:, None], target * weight, rcond=None)[0]


HALF = fit_half_angle()
TOP = float(2.0 * HALF[-1] ** 2)
SERIES = [float(term / HALF[-1]) for term in HALF]
LOW = 2.0**15
CLIP = 256.0
GRANT = 20


def split(values):
    high = values.astype(bf16)
    return high, (values - high.astype(f32)).astype(bf16)


def cosine(turns):
    rest = turns - jnp.round(turns)
    square = rest * rest
    series = square + SERIES[2]
    series = series * square + SERIES[1]
    series = series * square + SERIES[0]
    return series * series - 1.0 / TOP


def divisor(size, most):
    while size % most:
        most //= 2
    return most


def padded(factors, width):
    rows, risks = factors.shape
    ones = (lax.broadcasted_iota(jnp.int32, (rows, width - risks), 1) < 3).astype(f32)
    return jnp.concatenate([factors.astype(f32).astype(bf16), ones.astype(bf16)], 1)


def prepare_kernel(
    own_ref, freq_ref, phase_ref, amp_ref, coeffs_ref, factor_out, freq_out, start_out, amp_out,
    own_buf, freq_buf, phase_buf, amp_buf, coeffs_buf, whole_sem, freq_sem,
):
    risks = own_ref.shape[1]
    count = coeffs_ref.shape[0]
    steps, _, cols = freq_buf.shape
    extra = freq_out.shape[0] - risks
    first = lax.axis_index("paths") * cols * steps

    def fetch(index):
        source = pl.ds(pl.multiple_of(first + index * cols, cols), cols)
        return pltpu.make_async_copy(freq_ref.at[:, source], freq_buf.at[index], freq_sem.at[index])

    mine = pl.ds(pl.multiple_of(first, cols), cols * steps)
    wholes = [
        pltpu.make_async_copy(source, target, whole_sem.at[number])
        for number, (source, target) in enumerate(
            (
                (phase_ref.at[:, mine], phase_buf),
                (amp_ref.at[:, mine], amp_buf),
                (coeffs_ref.at[:, mine], coeffs_buf),
                (own_ref, own_buf),
            )
        )
    ]
    for copy in wholes:
        copy.start()
    for index in range(steps):
        fetch(index).start()
    for copy in wholes:
        copy.wait()
    factor_out[...] = padded(own_buf[...], factor_out.shape[1])
    row = lax.broadcasted_iota(jnp.int32, (extra, cols), 0)
    for index in range(steps):
        span = pl.ds(index * cols, cols)
        phase = phase_buf[:, span].astype(f32) * (1.0 / (1024.0 * TURN))
        piece_high = phase.astype(bf16).astype(f32)
        piece_middle = (phase - piece_high).astype(bf16).astype(f32)
        piece_low = phase - piece_high - piece_middle
        pieces = jnp.where(row == 0, piece_high, jnp.where(row == 1, piece_middle, jnp.where(row == 2, piece_low, 0.0)))
        freq_out[risks:, span] = pieces.astype(bf16)
        amp = amp_buf[:, span] * TOP
        amp_out[:, span] = amp
        start_high, start_low = split(coeffs_buf[:, span] * amp)
        start_out[:count, span] = start_high
        start_out[count:, span] = start_low
    for index in range(steps):
        fetch(index).wait()
        freq_out[:risks, pl.ds(index * cols, cols)] = freq_buf[index].astype(f32).astype(bf16)


def build_kernel(
    own_ref, other_ref, freq_ref, start_ref, blank_high, blank_low, image_own, image_other, high_ref, low_ref, other_buf
):
    paths, width = high_ref.shape
    half = paths // 2
    cols = divisor(width, 1024)
    rows = divisor(half, 512)
    count = start_ref.shape[0] // 2
    other_buf[...] = padded(other_ref[...], other_buf.shape[1])

    image_own[...] = jnp.zeros_like(image_own)
    image_other[...] = jnp.zeros_like(image_other)

    def block(index, carry):
        span = pl.ds(pl.multiple_of(index * cols, cols), cols)
        freq, start = freq_ref[:, span], start_ref[:, span]

        def sums_of(part):
            factor_ref = own_ref if part * rows < half else other_buf
            factors = factor_ref[pl.ds(part * rows % half, rows), :]
            return lax.dot_general(factors, freq, NN, preferred_element_type=f32)

        def add_image(part, high, low):
            main = lax.dot_general(start, high, NT, preferred_element_type=f32)
            rest = lax.dot_general(low, start[:count], NT, preferred_element_type=f32)
            image_ref = image_own if part * rows < half else image_other
            image_ref[:, pl.ds(part * rows % half, rows)] += main[:count] + main[count:] + rest.T

        parts = paths // rows
        summed = sums_of(0)
        before = None
        for part in range(parts):
            summed_after = sums_of(part + 1) if part + 1 < parts else None
            place = pl.ds(part * rows, rows)
            values = cosine(summed * TURN)
            high = values.astype(bf16)
            rest = values - high.astype(f32)
            high_ref[place, span] = high
            low_ref[place, span] = (rest * LOW).astype(f8)
            if before is not None:
                add_image(*before)
            before = part, high, rest.astype(bf16)
            summed = summed_after
        add_image(*before)
        return carry

    lax.fori_loop(0, width // cols, block, 0)


def gradient_of(clipped, high_ref, low_ref, place, span):
    count = clipped.shape[0]
    pair = jnp.concatenate(split(clipped), 0)
    main = lax.dot_general(pair, high_ref[place, span], NN, preferred_element_type=f32)
    coarse = (clipped * CLIP).astype(f8)
    rest = lax.dot_general(coarse, low_ref[place, span], NN, preferred_element_type=f32)
    return main[:count] + main[count:] + rest * (1.0 / (CLIP * LOW))


def image_of(pair_ref, coarse_ref, level, high_ref, low_ref, start, image_ref):
    count, half = pair_ref.shape[0] // 2, high_ref.shape[0] // 2
    rows = divisor(half, 512)
    for first in range(0, half, rows):
        place = pl.ds(start + first, rows)
        main = lax.dot_general(high_ref[place, :], pair_ref[...], NT, preferred_element_type=f32).T
        rest = lax.dot_general(coarse_ref[...], low_ref[place, :], NT, preferred_element_type=f32)
        image = main[:count] + main[count:] + rest * (level * (1.0 / LOW))
        for lane in range(0, rows, 128):
            image_ref[pl.ds((first + lane) // 128 * count, count), :] = image[:, lane : lane + 128]


def own_kernel(clipped_ref, high_ref, low_ref, partial_out):
    paths, width = high_ref.shape
    cols = divisor(width, 4096)
    for index in range(width // cols):
        span = pl.ds(index * cols, cols)
        partial_out[:, span] = gradient_of(clipped_ref[...], high_ref, low_ref, pl.ds(0, paths // 2), span)


def rest_kernel(
    clipped_ref, high_ref, low_ref, partial_ref, amp_ref, grad_out, pair_out, coarse_out, image_out, notes_out
):
    paths, width = high_ref.shape
    half = paths // 2
    count = clipped_ref.shape[0]
    cols = divisor(width, 4096)
    squares = jnp.zeros((8, 128), f32)
    largest = jnp.zeros((count, 128), f32)
    for index in range(width // cols):
        span = pl.ds(index * cols, cols)
        share = gradient_of(clipped_ref[...], high_ref, low_ref, pl.ds(half, half), span)
        amp = amp_ref[:, span]
        grad = (partial_ref[:, span] + share) * amp
        grad_out[:, span] = grad
        pushed = grad * amp
        high, low = split(pushed)
        pair_out[:count, span] = high
        pair_out[count:, span] = low
        for lane in range(0, cols, 128):
            largest = jnp.maximum(largest, jnp.abs(pushed[:, lane : lane + 128]))
            for row in range(0, count, 8):
                tile = grad[row : row + 8, lane : lane + 128]
                squares = squares + tile * tile
    level = jnp.maximum(jnp.max(largest, axis=1, keepdims=True), 1e-30) * (1.0 / 240.0)
    for index in range(width // cols):
        span = pl.ds(index * cols, cols)
        coarse_out[:, span] = (pair_out[:count, span].astype(f32) * (1.0 / level)).astype(f8)
    image_of(pair_out, coarse_out, level, high_ref, low_ref, half, image_out)
    image_out[pl.ds(count * half // 128, 8), :] = squares
    notes_out[:8, :] = squares
    notes_out[8:, :] = jnp.broadcast_to(level, (count, 128))


def image_kernel(pair_ref, coarse_ref, notes_ref, high_ref, low_ref, image_out):
    half = high_ref.shape[0] // 2
    image_of(pair_ref, coarse_ref, notes_ref[8:, :1], high_ref, low_ref, 0, image_out)
    image_out[pl.ds(pair_ref.shape[0] // 2 * half // 128, 8), :] = notes_ref[:8, :]


def start_kernel(own_ref, other_ref, front_out, back_out):
    count, half = own_ref.shape
    tiles = half // 128
    for tile in range(tiles):
        out = front_out if tile < tiles // 2 else back_out
        span = pl.ds(tile * 128, 128)
        out[pl.ds(tile % (tiles // 2) * count, count), :] = own_ref[:, span] + other_ref[:, span]


def join_kernel(own_ref, other_ref, front_out, back_out):
    middle, end = back_out.shape[0], 2 * back_out.shape[0]
    front_out[:middle, :] = own_ref[:middle, :] + other_ref[:middle, :]
    front_out[middle:, :] = own_ref[end:, :] + other_ref[end:, :]
    back_out[...] = own_ref[middle:end, :] + other_ref[middle:end, :]


def add_kernel(one_ref, other_ref, sum_ref):
    sum_ref[...] = one_ref[...] + other_ref[...]


def places(targets_ref, front, back):
    count, half = targets_ref.shape
    tiles = half // 128
    for tile in range(tiles):
        refs = front if tile < tiles // 2 else back
        yield pl.ds(tile * 128, 128), refs, pl.ds(tile % (tiles // 2) * count, count)


def open_kernel(front, front_last, back, back_last, targets_ref, clipped_out, predicted_out):
    for span, (one, other), rows in places(targets_ref, (front, front_last), (back, back_last)):
        predicted = one[rows, :] + other[rows, :]
        predicted_out[:, span] = predicted
        clipped_out[:, span] = jnp.clip(predicted - targets_ref[:, span], -huber_cap, huber_cap)


def inverse_of(entries, front, front_last, back):
    end = pl.ds(back.shape[0], 8)
    total = jnp.sum(front[end, :] + front_last[end, :], axis=(0, 1), keepdims=True)
    return 1.0 / jnp.sqrt(total / entries + epsilon)


def step_kernel(entries, front, front_last, back, back_last, targets_ref, predicted_ref, *refs):
    tracked_ref = refs[0] if len(refs) == 5 else None
    clipped_out, predicted_out, inverse_out, tracked_out = refs[-4:]
    inverse = inverse_of(entries, front, front_last, back)
    inverse_out[...] = jnp.broadcast_to(inverse, (8, 128))
    for span, (one, other), rows in places(targets_ref, (front, front_last), (back, back_last)):
        tracked = (one[rows, :] + other[rows, :]) * inverse
        if tracked_ref is not None:
            tracked = momentum * tracked_ref[:, span] + tracked
        predicted = predicted_ref[:, span] - step_rate * tracked
        tracked_out[:, span] = tracked
        predicted_out[:, span] = predicted
        clipped_out[:, span] = jnp.clip(predicted - targets_ref[:, span], -huber_cap, huber_cap)


def sum_kernel(weights, *refs):
    total = jnp.zeros_like(refs[-1])
    for weight, grad_ref, inverse_ref in zip(weights, refs[:-1:2], refs[1:-1:2]):
        total = total + (weight * inverse_ref[0:1, 0:1]) * grad_ref[...]
    refs[-1][...] = total


def close_kernel(entries, weight, front, front_last, back, back_last, targets_ref, predicted_ref, tracked_ref, *refs):
    coeffs_ref, taken_ref, other_taken, grad_ref, other_grad, predicted_out, coeffs_out = refs
    inverse = inverse_of(entries, front, front_last, back)
    for span, (one, other), rows in places(targets_ref, (front, front_last), (back, back_last)):
        tracked = momentum * tracked_ref[:, span] + (one[rows, :] + other[rows, :]) * inverse
        predicted_out[:, span] = predicted_ref[:, span] - step_rate * tracked
    width = taken_ref.shape[1]
    core = lax.axis_index("paths")
    factor = weight * inverse
    for start, taken, grad in ((core, taken_ref, grad_ref), (1 - core, other_taken, other_grad)):
        span = pl.ds(pl.multiple_of(start * width, width), width)
        coeffs_out[:, span] = coeffs_ref[:, span] - (taken[...] + factor * grad[...])


def vmem(count):
    return [pl.BlockSpec(memory_space=pltpu.VMEM)] * count


def held(array):
    return pltpu.with_memory_space_constraint(array, pltpu.VMEM)


def call(kernel, name, arguments, shapes, specs=None, scratch=(), megabytes=4, aliases={}):
    shapes = tuple(shape if not isinstance(shape, tuple) else jax.ShapeDtypeStruct(shape, f32) for shape in shapes)
    return pl.pallas_call(
        kernel,
        out_shape=shapes,
        in_specs=specs or vmem(len(arguments)),
        out_specs=tuple(vmem(len(shapes))),
        scratch_shapes=scratch,
        compiler_params=pltpu.CompilerParams(vmem_limit_bytes=megabytes * 2**20),
        input_output_aliases=aliases,
        name=name,
    )(*arguments)


def shards(sizes, factors, frequency, phases, amplitude, targets, coeffs_init):
    cores, chips = sizes["paths"], sizes["feats"]
    half, risks = factors.shape
    width = frequency.shape[1] // cores
    count = targets.shape[0]
    paths = half * cores
    entries = count * width * cores * chips
    hops = [1 << bit for bit in range(chips.bit_length() - 1)]

    def swap(array):
        return lax.ppermute(array, "paths", [(0, 1), (1, 0)])

    def add(one, other):
        return call(add_kernel, "add", (one, other), (one.shape,))[0]

    def all_chips(front, back):
        orders = hops, hops[1::-1] + hops[2:]
        sums = [front, back]
        for step in range(len(hops)):
            lasts = [
                lax.ppermute(array, "feats", [(chip, chip ^ order[step]) for chip in range(chips)])
                for array, order in zip(sums, orders)
            ]
            if step < len(hops) - 1:
                sums = [add(array, last) for array, last in zip(sums, lasts)]
        return sums[0], lasts[0], sums[1], lasts[1]

    small, wide, row = (count, half), (count, width), (1, width)
    extent = count * half // 128
    middle = extent // 2
    features = pltpu.VMEM((paths, width), bf16), pltpu.VMEM((paths, width), f8)
    blanks = [
        pl.pallas_call(
            lambda out: None,
            out_shape=feature,
            out_specs=vmem(1)[0],
            compiler_params=pltpu.CompilerParams(vmem_limit_bytes=2**20),
            name=name,
        )()
        for name, feature in zip(("blank_high", "blank_low"), features)
    ]
    deep, cols = 2 * risks, divisor(width, 1024)
    own_factors, freq, start, amp = call(
        prepare_kernel,
        "prepare",
        [
            pltpu.with_memory_space_constraint(array, pltpu.HBM)
            for array in (factors, frequency, phases[None], amplitude[None], coeffs_init)
        ],
        (
            jax.ShapeDtypeStruct((half, deep), bf16),
            jax.ShapeDtypeStruct((deep, width), bf16),
            jax.ShapeDtypeStruct((2 * count, width), bf16),
            row,
        ),
        [pl.BlockSpec(memory_space=pltpu.HBM)] * 5,
        [
            pltpu.VMEM(factors.shape, factors.dtype),
            pltpu.VMEM((width // cols, risks, cols), frequency.dtype),
            pltpu.VMEM(row, phases.dtype),
            pltpu.VMEM(row, f32),
            pltpu.VMEM(wide, f32),
            pltpu.SemaphoreType.DMA((4,)),
            pltpu.SemaphoreType.DMA((width // cols,)),
        ],
        12,
    )
    image_own, image_other, high, low = call(
        build_kernel,
        "build",
        (own_factors, swap(factors), freq, start, held(blanks[0]), held(blanks[1])),
        (small, small, *features),
        None,
        [pltpu.VMEM((half, deep), bf16)],
        GRANT,
        {4: 2, 5: 3},
    )
    sums = all_chips(*call(start_kernel, "start", (image_own, swap(image_other)), ((middle, 128), (middle, 128))))
    clipped, predicted = call(open_kernel, "open", (*sums, targets), (small, small))
    weights = [step_rate * sum(momentum**later for later in range(ITERS - turn)) for turn in range(ITERS)]
    tracked = ()
    grads, inverses = [], []
    for turn in range(ITERS):
        partial = call(own_kernel, "own", (clipped, held(high), held(low)), (wide,), None, (), GRANT)[0]
        pieces = jax.ShapeDtypeStruct((2 * count, width), bf16), jax.ShapeDtypeStruct(wide, f8)
        grad, pair, coarse, image_other, notes = call(
            rest_kernel,
            "rest",
            (swap(clipped), held(high), held(low), partial, amp),
            (wide, *pieces, (extent + 8, 128), (count + 8, 128)),
            None,
            (),
            GRANT,
        )
        image_own = call(
            image_kernel, "image", (pair, coarse, notes, held(high), held(low)), ((extent + 8, 128),), None, (), GRANT
        )[0]
        halves = call(join_kernel, "join", (image_own, swap(image_other)), ((middle + 8, 128), (middle, 128)))
        grads.append(grad)
        if turn == ITERS - 1:
            break
        clipped, predicted, inverse, *tracked = call(
            functools.partial(step_kernel, entries),
            "step",
            (*all_chips(*halves), targets, predicted, *tracked),
            (small, small, (8, 128), small),
        )
        inverses.append(inverse)
    before = [array for pair in zip(grads, inverses) for array in pair]
    taken = call(functools.partial(sum_kernel, weights[:-1]), "sum", before, (wide,))[0]
    predicted, coeffs = call(
        functools.partial(close_kernel, entries, weights[-1]),
        "close",
        (*all_chips(*halves), targets, predicted, *tracked, coeffs_init, taken, swap(taken), grad, swap(grad)),
        (small, (count, width * cores)),
        None,
        (),
        8,
    )
    return (coeffs, predicted)


def solution(mesh):
    return jax.shard_map(
        functools.partial(shards, dict(mesh.shape)),
        mesh=mesh,
        in_specs=(
            P(("groups", "paths"), None),
            P(None, "feats"),
            P("feats"),
            P("feats"),
            P(None, ("groups", "paths")),
            P(None, ("groups", "feats")),
        ),
        out_specs=(P(None, ("groups", "feats")), P(None, ("groups", "paths"))),
        check_vma=False,
    )
```

```python
import functools
import math

import jax
import jax.numpy as jnp
import numpy as np
from jax import lax
from jax.experimental import pallas as pl
from jax.experimental.pallas import tpu as pltpu
from jax.sharding import PartitionSpec as P

ITERS = 3

huber_cap = 1.0
step_rate = 0.2
momentum = 0.9
epsilon = 1e-06

f32 = jnp.float32
bf16 = jnp.bfloat16
f8 = jnp.float8_e4m3fn
NN = (((1,), (0,)), ((), ()))
NT = (((1,), (1,)), ((), ()))
TURN = 0.0025 / (2.0 * math.pi)


def fit_half_angle():
    rest = np.cos(np.linspace(0, np.pi, 4001)) * 0.5
    target = np.cos(np.pi * rest)
    basis = np.stack([rest ** (2 * i) for i in range(4)], 1)
    weight = np.abs(target) + 1e-3
    return np.linalg.lstsq(basis * weight[:, None], target * weight, rcond=None)[0]


HALF = fit_half_angle()
TOP = float(2.0 * HALF[-1] ** 2)
SERIES = [float(term / HALF[-1]) for term in HALF]
LOW = 2.0**15
CLIP = 256.0
GRANT = 20


def split(values):
    high = values.astype(bf16)
    return high, (values - high.astype(f32)).astype(bf16)


def cosine(turns):
    rest = turns - jnp.round(turns)
    square = rest * rest
    series = square + SERIES[2]
    series = series * square + SERIES[1]
    series = series * square + SERIES[0]
    return series * series - 1.0 / TOP


def divisor(size, most):
    while size % most:
        most //= 2
    return most


def padded(factors, width):
    rows, risks = factors.shape
    ones = (lax.broadcasted_iota(jnp.int32, (rows, width - risks), 1) < 3).astype(f32)
    return jnp.concatenate([factors.astype(f32).astype(bf16), ones.astype(bf16)], 1)


def prepare_kernel(
    own_ref, freq_ref, phase_ref, amp_ref, coeffs_ref, factor_out, freq_out, start_out, amp_out,
    own_buf, freq_buf, phase_buf, amp_buf, coeffs_buf, whole_sem, freq_sem,
):
    risks = own_ref.shape[1]
    count = coeffs_ref.shape[0]
    steps, _, cols = freq_buf.shape
    extra = freq_out.shape[0] - risks
    first = lax.axis_index("paths") * cols * steps

    def fetch(index):
        source = pl.ds(pl.multiple_of(first + index * cols, cols), cols)
        return pltpu.make_async_copy(freq_ref.at[:, source], freq_buf.at[index], freq_sem.at[index])

    mine = pl.ds(pl.multiple_of(first, cols), cols * steps)
    wholes = [
        pltpu.make_async_copy(source, target, whole_sem.at[number])
        for number, (source, target) in enumerate(
            (
                (phase_ref.at[:, mine], phase_buf),
                (amp_ref.at[:, mine], amp_buf),
                (coeffs_ref.at[:, mine], coeffs_buf),
                (own_ref, own_buf),
            )
        )
    ]
    for copy in wholes:
        copy.start()
    for index in range(steps):
        fetch(index).start()
    for copy in wholes:
        copy.wait()
    factor_out[...] = padded(own_buf[...], factor_out.shape[1])
    row = lax.broadcasted_iota(jnp.int32, (extra, cols), 0)
    for index in range(steps):
        span = pl.ds(index * cols, cols)
        phase = phase_buf[:, span].astype(f32) * (1.0 / (1024.0 * TURN))
        piece_high = phase.astype(bf16).astype(f32)
        piece_middle = (phase - piece_high).astype(bf16).astype(f32)
        piece_low = phase - piece_high - piece_middle
        pieces = jnp.where(row == 0, piece_high, jnp.where(row == 1, piece_middle, jnp.where(row == 2, piece_low, 0.0)))
        freq_out[risks:, span] = pieces.astype(bf16)
        amp = amp_buf[:, span] * TOP
        amp_out[:, span] = amp
        start_high, start_low = split(coeffs_buf[:, span] * amp)
        start_out[:count, span] = start_high
        start_out[count:, span] = start_low
    for index in range(steps):
        fetch(index).wait()
        freq_out[:risks, pl.ds(index * cols, cols)] = freq_buf[index].astype(f32).astype(bf16)


def build_kernel(
    own_ref, other_ref, freq_ref, start_ref, blank_high, blank_low, image_own, image_other, high_ref, low_ref, other_buf
):
    paths, width = high_ref.shape
    half = paths // 2
    cols = divisor(width, 1024)
    rows = divisor(half, 512)
    count = start_ref.shape[0] // 2
    other_buf[...] = padded(other_ref[...], other_buf.shape[1])

    image_own[...] = jnp.zeros_like(image_own)
    image_other[...] = jnp.zeros_like(image_other)

    def block(index, carry):
        span = pl.ds(pl.multiple_of(index * cols, cols), cols)
        freq, start = freq_ref[:, span], start_ref[:, span]

        def sums_of(part):
            factor_ref = own_ref if part * rows < half else other_buf
            factors = factor_ref[pl.ds(part * rows % half, rows), :]
            return lax.dot_general(factors, freq, NN, preferred_element_type=f32)

        def add_image(part, high, low):
            main = lax.dot_general(start, high, NT, preferred_element_type=f32)
            rest = lax.dot_general(low, start[:count], NT, preferred_element_type=f32)
            image_ref = image_own if part * rows < half else image_other
            image_ref[:, pl.ds(part * rows % half, rows)] += main[:count] + main[count:] + rest.T

        parts = paths // rows
        summed = sums_of(0)
        before = None
        for part in range(parts):
            summed_after = sums_of(part + 1) if part + 1 < parts else None
            place = pl.ds(part * rows, rows)
            values = cosine(summed * TURN)
            high = values.astype(bf16)
            rest = values - high.astype(f32)
            high_ref[place, span] = high
            low_ref[place, span] = (rest * LOW).astype(f8)
            if before is not None:
                add_image(*before)
            before = part, high, rest.astype(bf16)
            summed = summed_after
        add_image(*before)
        return carry

    lax.fori_loop(0, width // cols, block, 0)


def gradient_of(clipped, high_ref, low_ref, place, span):
    count = clipped.shape[0]
    pair = jnp.concatenate(split(clipped), 0)
    main = lax.dot_general(pair, high_ref[place, span], NN, preferred_element_type=f32)
    coarse = (clipped * CLIP).astype(f8)
    rest = lax.dot_general(coarse, low_ref[place, span], NN, preferred_element_type=f32)
    return main[:count] + main[count:] + rest * (1.0 / (CLIP * LOW))


def image_of(pair_ref, coarse_ref, level, high_ref, low_ref, start, image_ref):
    count, half = pair_ref.shape[0] // 2, high_ref.shape[0] // 2
    rows = divisor(half, 512)
    for first in range(0, half, rows):
        place = pl.ds(start + first, rows)
        main = lax.dot_general(high_ref[place, :], pair_ref[...], NT, preferred_element_type=f32).T
        rest = lax.dot_general(coarse_ref[...], low_ref[place, :], NT, preferred_element_type=f32)
        image = main[:count] + main[count:] + rest * (level * (1.0 / LOW))
        for lane in range(0, rows, 128):
            image_ref[pl.ds((first + lane) // 128 * count, count), :] = image[:, lane : lane + 128]


def own_kernel(clipped_ref, high_ref, low_ref, partial_out):
    paths, width = high_ref.shape
    cols = divisor(width, 4096)
    for index in range(width // cols):
        span = pl.ds(index * cols, cols)
        partial_out[:, span] = gradient_of(clipped_ref[...], high_ref, low_ref, pl.ds(0, paths // 2), span)


def rest_kernel(
    clipped_ref, high_ref, low_ref, partial_ref, amp_ref, grad_out, pair_out, coarse_out, image_out, notes_out
):
    paths, width = high_ref.shape
    half = paths // 2
    count = clipped_ref.shape[0]
    cols = divisor(width, 4096)
    squares = jnp.zeros((8, 128), f32)
    largest = jnp.zeros((count, 128), f32)
    for index in range(width // cols):
        span = pl.ds(index * cols, cols)
        share = gradient_of(clipped_ref[...], high_ref, low_ref, pl.ds(half, half), span)
        amp = amp_ref[:, span]
        grad = (partial_ref[:, span] + share) * amp
        grad_out[:, span] = grad
        pushed = grad * amp
        high, low = split(pushed)
        pair_out[:count, span] = high
        pair_out[count:, span] = low
        for lane in range(0, cols, 128):
            largest = jnp.maximum(largest, jnp.abs(pushed[:, lane : lane + 128]))
            for row in range(0, count, 8):
                tile = grad[row : row + 8, lane : lane + 128]
                squares = squares + tile * tile
    level = jnp.maximum(jnp.max(largest, axis=1, keepdims=True), 1e-30) * (1.0 / 240.0)
    for index in range(width // cols):
        span = pl.ds(index * cols, cols)
        coarse_out[:, span] = (pair_out[:count, span].astype(f32) * (1.0 / level)).astype(f8)
    image_of(pair_out, coarse_out, level, high_ref, low_ref, half, image_out)
    image_out[pl.ds(count * half // 128, 8), :] = squares
    notes_out[:8, :] = squares
    notes_out[8:, :] = jnp.broadcast_to(level, (count, 128))


def image_kernel(pair_ref, coarse_ref, notes_ref, high_ref, low_ref, image_out):
    half = high_ref.shape[0] // 2
    image_of(pair_ref, coarse_ref, notes_ref[8:, :1], high_ref, low_ref, 0, image_out)
    image_out[pl.ds(pair_ref.shape[0] // 2 * half // 128, 8), :] = notes_ref[:8, :]


def start_kernel(own_ref, other_ref, front_out, back_out):
    count, half = own_ref.shape
    tiles = half // 128
    for tile in range(tiles):
        out = front_out if tile < tiles // 2 else back_out
        span = pl.ds(tile * 128, 128)
        out[pl.ds(tile % (tiles // 2) * count, count), :] = own_ref[:, span] + other_ref[:, span]


def join_kernel(own_ref, other_ref, front_out, back_out):
    middle, end = back_out.shape[0], 2 * back_out.shape[0]
    front_out[:middle, :] = own_ref[:middle, :] + other_ref[:middle, :]
    front_out[middle:, :] = own_ref[end:, :] + other_ref[end:, :]
    back_out[...] = own_ref[middle:end, :] + other_ref[middle:end, :]


def add_kernel(one_ref, other_ref, sum_ref):
    sum_ref[...] = one_ref[...] + other_ref[...]


def places(targets_ref, front, back):
    count, half = targets_ref.shape
    tiles = half // 128
    for tile in range(tiles):
        refs = front if tile < tiles // 2 else back
        yield pl.ds(tile * 128, 128), refs, pl.ds(tile % (tiles // 2) * count, count)


def open_kernel(front, front_last, back, back_last, targets_ref, clipped_out, predicted_out):
    for span, (one, other), rows in places(targets_ref, (front, front_last), (back, back_last)):
        predicted = one[rows, :] + other[rows, :]
        predicted_out[:, span] = predicted
        clipped_out[:, span] = jnp.clip(predicted - targets_ref[:, span], -huber_cap, huber_cap)


def inverse_of(entries, front, front_last, start):
    end = pl.ds(start, 8)
    total = jnp.sum(front[end, :] + front_last[end, :], axis=(0, 1), keepdims=True)
    return 1.0 / jnp.sqrt(total / entries + epsilon)


def step_kernel(entries, front, front_last, back, back_last, targets_ref, predicted_ref, *refs):
    tracked_ref = refs[0] if len(refs) == 5 else None
    clipped_out, predicted_out, inverse_out, tracked_out = refs[-4:]
    inverse = inverse_of(entries, front, front_last, back.shape[0])
    inverse_out[...] = jnp.broadcast_to(inverse, (8, 128))
    for span, (one, other), rows in places(targets_ref, (front, front_last), (back, back_last)):
        tracked = (one[rows, :] + other[rows, :]) * inverse
        if tracked_ref is not None:
            tracked = momentum * tracked_ref[:, span] + tracked
        predicted = predicted_ref[:, span] - step_rate * tracked
        tracked_out[:, span] = tracked
        predicted_out[:, span] = predicted
        clipped_out[:, span] = jnp.clip(predicted - targets_ref[:, span], -huber_cap, huber_cap)


def sum_kernel(weights, *refs):
    total = jnp.zeros_like(refs[-1])
    for weight, grad_ref, inverse_ref in zip(weights, refs[:-1:2], refs[1:-1:2]):
        total = total + (weight * inverse_ref[0:1, 0:1]) * grad_ref[...]
    refs[-1][...] = total


def close_kernel(entries, weight, front, front_last, *refs):
    coeffs_ref, taken_ref, other_taken, grad_ref, other_grad, coeffs_out, inverse_out = refs
    inverse = inverse_of(entries, front, front_last, front.shape[0] - 8)
    inverse_out[...] = jnp.broadcast_to(inverse, (8, 128))
    width = taken_ref.shape[1]
    core = lax.axis_index("paths")
    factor = weight * inverse
    for start, taken, grad in ((core, taken_ref, grad_ref), (1 - core, other_taken, other_grad)):
        span = pl.ds(pl.multiple_of(start * width, width), width)
        coeffs_out[:, span] = coeffs_ref[:, span] - (taken[...] + factor * grad[...])


def last_kernel(front, front_last, back, back_last, predicted_ref, tracked_ref, inverse_ref, predicted_out):
    inverse = inverse_ref[0:1, 0:1]
    for span, (one, other), rows in places(predicted_ref, (front, front_last), (back, back_last)):
        tracked = momentum * tracked_ref[:, span] + (one[rows, :] + other[rows, :]) * inverse
        predicted_out[:, span] = predicted_ref[:, span] - step_rate * tracked


def vmem(count):
    return [pl.BlockSpec(memory_space=pltpu.VMEM)] * count


def held(array):
    return pltpu.with_memory_space_constraint(array, pltpu.VMEM)


def call(kernel, name, arguments, shapes, specs=None, scratch=(), megabytes=4, aliases={}):
    shapes = tuple(shape if not isinstance(shape, tuple) else jax.ShapeDtypeStruct(shape, f32) for shape in shapes)
    return pl.pallas_call(
        kernel,
        out_shape=shapes,
        in_specs=specs or vmem(len(arguments)),
        out_specs=tuple(vmem(len(shapes))),
        scratch_shapes=scratch,
        compiler_params=pltpu.CompilerParams(vmem_limit_bytes=megabytes * 2**20),
        input_output_aliases=aliases,
        name=name,
    )(*arguments)


def shards(sizes, factors, frequency, phases, amplitude, targets, coeffs_init):
    cores, chips = sizes["paths"], sizes["feats"]
    half, risks = factors.shape
    width = frequency.shape[1] // cores
    count = targets.shape[0]
    paths = half * cores
    entries = count * width * cores * chips
    hops = [1 << bit for bit in range(chips.bit_length() - 1)]

    def swap(array):
        return lax.ppermute(array, "paths", [(0, 1), (1, 0)])

    def add(one, other):
        return call(add_kernel, "add", (one, other), (one.shape,))[0]

    def all_chips(front, back):
        orders = hops, hops[1::-1] + hops[2:]
        sums = [front, back]
        for step in range(len(hops)):
            lasts = [
                lax.ppermute(array, "feats", [(chip, chip ^ order[step]) for chip in range(chips)])
                for array, order in zip(sums, orders)
            ]
            if step < len(hops) - 1:
                sums = [add(array, last) for array, last in zip(sums, lasts)]
        return sums[0], lasts[0], sums[1], lasts[1]

    small, wide, row = (count, half), (count, width), (1, width)
    extent = count * half // 128
    middle = extent // 2
    features = pltpu.VMEM((paths, width), bf16), pltpu.VMEM((paths, width), f8)
    blanks = [
        pl.pallas_call(
            lambda out: None,
            out_shape=feature,
            out_specs=vmem(1)[0],
            compiler_params=pltpu.CompilerParams(vmem_limit_bytes=2**20),
            name=name,
        )()
        for name, feature in zip(("blank_high", "blank_low"), features)
    ]
    deep, cols = 2 * risks, divisor(width, 1024)
    own_factors, freq, start, amp = call(
        prepare_kernel,
        "prepare",
        [
            pltpu.with_memory_space_constraint(array, pltpu.HBM)
            for array in (factors, frequency, phases[None], amplitude[None], coeffs_init)
        ],
        (
            jax.ShapeDtypeStruct((half, deep), bf16),
            jax.ShapeDtypeStruct((deep, width), bf16),
            jax.ShapeDtypeStruct((2 * count, width), bf16),
            row,
        ),
        [pl.BlockSpec(memory_space=pltpu.HBM)] * 5,
        [
            pltpu.VMEM(factors.shape, factors.dtype),
            pltpu.VMEM((width // cols, risks, cols), frequency.dtype),
            pltpu.VMEM(row, phases.dtype),
            pltpu.VMEM(row, f32),
            pltpu.VMEM(wide, f32),
            pltpu.SemaphoreType.DMA((4,)),
            pltpu.SemaphoreType.DMA((width // cols,)),
        ],
        12,
    )
    image_own, image_other, high, low = call(
        build_kernel,
        "build",
        (own_factors, swap(factors), freq, start, held(blanks[0]), held(blanks[1])),
        (small, small, *features),
        None,
        [pltpu.VMEM((half, deep), bf16)],
        GRANT,
        {4: 2, 5: 3},
    )
    sums = all_chips(*call(start_kernel, "start", (image_own, swap(image_other)), ((middle, 128), (middle, 128))))
    clipped, predicted = call(open_kernel, "open", (*sums, targets), (small, small))
    weights = [step_rate * sum(momentum**later for later in range(ITERS - turn)) for turn in range(ITERS)]
    tracked = ()
    grads, inverses = [], []
    for turn in range(ITERS):
        partial = call(own_kernel, "own", (clipped, held(high), held(low)), (wide,), None, (), GRANT)[0]
        pieces = jax.ShapeDtypeStruct((2 * count, width), bf16), jax.ShapeDtypeStruct(wide, f8)
        grad, pair, coarse, image_other, notes = call(
            rest_kernel,
            "rest",
            (swap(clipped), held(high), held(low), partial, amp),
            (wide, *pieces, (extent + 8, 128), (count + 8, 128)),
            None,
            (),
            GRANT,
        )
        image_own = call(
            image_kernel, "image", (pair, coarse, notes, held(high), held(low)), ((extent + 8, 128),), None, (), GRANT
        )[0]
        halves = call(join_kernel, "join", (image_own, swap(image_other)), ((middle + 8, 128), (middle, 128)))
        grads.append(grad)
        if turn == ITERS - 1:
            sums = all_chips(*halves)
            break
        clipped, predicted, inverse, *tracked = call(
            functools.partial(step_kernel, entries),
            "step",
            (*all_chips(*halves), targets, predicted, *tracked),
            (small, small, (8, 128), small),
        )
        inverses.append(inverse)
    before = [array for pair in zip(grads, inverses) for array in pair]
    taken = call(functools.partial(sum_kernel, weights[:-1]), "sum", before, (wide,))[0]
    coeffs, inverse = call(
        functools.partial(close_kernel, entries, weights[-1]),
        "close",
        (*sums[:2], coeffs_init, taken, swap(taken), grad, swap(grad)),
        ((count, width * cores), (8, 128)),
        None,
        (),
        8,
    )
    predicted = call(last_kernel, "last", (*sums, predicted, *tracked, inverse), (small,))[0]
    return (coeffs, predicted)


def solution(mesh):
    return jax.shard_map(
        functools.partial(shards, dict(mesh.shape)),
        mesh=mesh,
        in_specs=(
            P(("groups", "paths"), None),
            P(None, "feats"),
            P("feats"),
            P("feats"),
            P(None, ("groups", "paths")),
            P(None, ("groups", "feats")),
        ),
        out_specs=(P(None, ("groups", "feats")), P(None, ("groups", "paths"))),
        check_vma=False,
    )
```
